128 devices in a mesh: chan: 16 (over y, z_lo, core), row: 8 (over z_hi, x).
Axes of the slice: x: 4, y: 4, z: 4 (z_hi: 2, z_lo: 2; z = z_hi * 2 + z_lo), core: 2. Of those that a mesh axis runs over, the one named last changes fastest.
Arguments:
- pair: bfloat16 [1280, 1280, 128], P('row', 'chan'), may hold values from -6 to 6
- in_gain: float32 [128], replicated, may hold values from 0.1 to 1.9
- in_bias: float32 [128], replicated, may hold values from -3 to 3
- edge_weight: bfloat16 [128, 512], replicated, may hold values from -0.5 to 0.5
- gate_weight: bfloat16 [128, 128], replicated, may hold values from -0.5 to 0.5
- out_gain: float32 [128], replicated, may hold values from 0.1 to 1.9
- out_bias: float32 [128], replicated, may hold values from -3 to 3
- out_weight: bfloat16 [128, 128], replicated, may hold values from -0.5 to 0.5
Outputs:
- update: bfloat16 [1280, 1280, 128], P('row', 'chan')
The draws below stay inside these ranges and needn't reach their ends.
All inputs are finite; a program needn't handle non-finite values.
Results may differ from the reference program's by a relative error of at most 0.012.
Values may be sent and summed in bfloat16 or wider, within the bound.
No kernel may reach another device: no remote copies, remote signals or barrier semaphores. Data moves between devices by JAX's collectives and lax.ppermute only.
A program may use at most 128 MiB of HBM per device.

```python
import jax
import jax.numpy as jnp
from jax import lax

C = 128
H = 128
CROP = 1280
HG = 8
N_CHAN = 16


def block_levels(stream_key, extent, split, least, high):
    level, own = 1.0, jax.random.fold_in(stream_key, 6)
    for position, blocks in split:
        steps = jnp.exp(jax.random.uniform(jax.random.fold_in(own, position), (blocks,), jnp.float32, least / len(split), high / len(split)))
        level = level * jnp.repeat(steps, extent[position] // blocks).reshape([-1 if axis == position else 1 for axis in range(len(extent))])
    return level


def noise(stream_key, extent, spread, limit, pieces=(), held_as=jnp.bfloat16):
    factor_of = block_levels(stream_key, extent, pieces, -0.22, 0.18) if pieces else 1.0
    entries = jax.random.normal(stream_key, extent, jnp.float32) * spread * factor_of
    return jnp.minimum(jnp.maximum(entries, -limit), limit).astype(held_as)


def setup_inputs(seed: int = 0) -> dict:
    seeds = jax.random.split(jax.random.key(seed), 9)
    return {
        "pair": noise(seeds[0], (CROP, CROP, C), 1.0, 6.0, ((0, 8), (1, 16))),
        "in_gain": jnp.clip(1.0 + 0.18 * jax.random.normal(seeds[1], (C,), jnp.float32), 0.1, 1.9),
        "in_bias": noise(seeds[2], (C,), 0.5, 3.0, (), jnp.float32),
        "edge_weight": noise(seeds[3], (C, 4 * H), C ** -0.5, 0.5),
        "gate_weight": noise(seeds[4], (C, C), C ** -0.5, 0.5),
        "out_gain": jnp.clip(1.0 + 0.18 * jax.random.normal(seeds[5], (H,), jnp.float32), 0.1, 1.9),
        "out_bias": noise(seeds[6], (H,), 0.5, 3.0, (), jnp.float32),
        "out_weight": noise(seeds[7], (H, C), H ** -0.5, 0.5),
    }


def layer_norm(values, gain, bias, axis):
    mean = lax.optimization_barrier(jnp.mean(values, axis=axis, keepdims=True))
    centred = values - mean
    var = lax.optimization_barrier(jnp.mean(centred * centred, axis=axis, keepdims=True))
    return centred * lax.rsqrt(var + 1e-05) * gain + bias

def reference(pair, in_gain, in_bias, edge_weight, gate_weight, out_gain, out_bias, out_weight):
    normed = layer_norm(pair.astype(jnp.float32), in_gain, in_bias, -1).astype(jnp.bfloat16)
    flat = normed.reshape(CROP * CROP, C)

    def project(index):
        return jnp.dot(flat, edge_weight[:, index * H:(index + 1) * H], preferred_element_type=jnp.float32)
    left = (jax.nn.sigmoid(project(1)) * project(0)).astype(jnp.bfloat16)
    right = (jax.nn.sigmoid(project(3)) * project(2)).astype(jnp.bfloat16)
    gate = jax.nn.sigmoid(jnp.dot(flat, gate_weight, preferred_element_type=jnp.float32)).astype(jnp.bfloat16)
    left_major = left.reshape(CROP, CROP, HG * N_CHAN).transpose(2, 0, 1).reshape(N_CHAN, HG, CROP, CROP)
    right_major = right.reshape(CROP, CROP, HG * N_CHAN).transpose(2, 0, 1).reshape(N_CHAN, HG, CROP, CROP)

    def group(operands):
        lefts, rights = operands
        return jnp.einsum('cik,cjk->cij', lefts.astype(jnp.float32), rights.astype(jnp.float32)).astype(jnp.bfloat16)
    tri = lax.map(group, (left_major, right_major)).reshape(H, CROP, CROP)
    tri_normed = layer_norm(tri.astype(jnp.float32), out_gain[:, None, None], out_bias[:, None, None], 0).astype(jnp.bfloat16)
    projected = jnp.dot(tri_normed.reshape(H, CROP * CROP).T, out_weight, preferred_element_type=jnp.float32)
    return (gate.astype(jnp.float32) * projected).astype(jnp.bfloat16).reshape(CROP, CROP, C)
```

```python
import jax
import jax.numpy as jnp
from jax import lax
from jax.experimental import pallas as pl
from jax.experimental.pallas import tpu as pltpu
from jax.sharding import PartitionSpec as P

ROWS, COLS, C = 160, 80, 128
LANES = 128
REST = ROWS - LANES
PACK = LANES // REST
TAIL = COLS // PACK
CHUNK = 16
BOTH = 2 * (COLS + TAIL)
BACK = 104
N_ROW, N_CHAN = 8, 16
SIDE = 1280
F32, BF16 = jnp.float32, jnp.bfloat16
MIB = 1 << 20


def sigmoid(x):
    return 0.5 * jnp.tanh(0.5 * x) + 0.5


def layer_norm(values, gain, bias, axis):
    mean = jnp.mean(values, axis=axis, keepdims=True)
    centred = values - mean
    var = jnp.mean(centred * centred, axis=axis, keepdims=True)
    return centred * lax.rsqrt(var + 1e-05) * gain + bias


def edges_kernel(pair_ref, gain_ref, bias_ref, weight_ref, out_ref, weight_t, normed, dense, tail):
    step = pl.program_id(0)

    @pl.when(step == 0)
    def _():
        for m in range(4):
            weight_t[m * 128 : (m + 1) * 128, :] = weight_ref[:, m * 128 : (m + 1) * 128].T

    group = 8
    gain, bias = gain_ref[...], bias_ref[...]

    @pl.loop(0, ROWS // group)
    def _(n):
        block = pair_ref[pl.ds(n * group, group)].reshape(group * CHUNK, C).astype(F32)
        at = pl.multiple_of(n * group * CHUNK, group * CHUNK)
        normed[pl.ds(at, group * CHUNK), :] = layer_norm(block, gain, bias, -1)

    def product(x, side):
        both = lax.dot_general(
            weight_t[side * 256 : (side + 1) * 256, :], x, (((1,), (1,)), ((), ())), preferred_element_type=F32
        )
        return sigmoid(both[128:]) * both[:128]

    @pl.loop(0, CHUNK // 2)
    def _(n):
        x = jnp.concatenate(
            [normed[pl.ds(2 * n + e, LANES, stride=CHUNK), :] for e in range(2)], axis=0
        ).astype(BF16)
        for side in range(2):
            value = product(x, side)
            for e in range(2):
                dense[side, pl.ds(2 * n + e, C, stride=CHUNK), :] = value[:, e * 128 : (e + 1) * 128]

    for n in range(2):
        x = jnp.concatenate(
            [
                normed[pl.ds(LANES * CHUNK + 8 * n + e, REST, stride=CHUNK), :]
                for e in range(8)
            ],
            axis=0,
        ).astype(BF16)
        for side in range(2):
            value = product(x, side)
            for e in range(2):
                tail[pl.ds(side * TAIL + 4 * step + 2 * n + e, C, stride=2 * TAIL), :] = value[:, e * 128 : (e + 1) * 128]

    @pl.loop(0, C // 8)
    def _(n):
        at = pl.multiple_of(n * 8 * CHUNK, 8 * CHUNK)
        for side in range(2):
            to = pl.multiple_of(side * COLS + step * CHUNK, CHUNK)
            out_ref[pl.ds(8 * n, 8), pl.ds(to, CHUNK), :] = (
                dense[side, pl.ds(at, 8 * CHUNK), :].reshape(8, CHUNK, LANES).astype(BF16)
            )

    @pl.when(step == COLS // CHUNK - 1)
    def _():
        @pl.loop(0, C // 8)
        def _(n):
            at = pl.multiple_of(n * 16 * TAIL, 16 * TAIL)
            out_ref[pl.ds(8 * n, 8), 2 * COLS :, :] = (
                tail[pl.ds(at, 16 * TAIL), :].reshape(8, 2 * TAIL, LANES).astype(BF16)
            )


def edges(pair, gain, bias, weight):
    return pl.pallas_call(
        edges_kernel,
        grid=(COLS // CHUNK,),
        in_specs=[
            pl.BlockSpec((ROWS, CHUNK, C), lambda t: (0, t, 0)),
            pl.BlockSpec((1, C), lambda t: (0, 0)),
            pl.BlockSpec((1, C), lambda t: (0, 0)),
            pl.BlockSpec((C, 4 * C), lambda t: (0, 0)),
        ],
        out_specs=pl.BlockSpec((C, BOTH, LANES), lambda t: (0, 0, 0)),
        out_shape=jax.ShapeDtypeStruct((C, BOTH, LANES), BF16),
        scratch_shapes=[
            pltpu.VMEM((4 * C, C), BF16),
            pltpu.VMEM((ROWS * CHUNK, C), F32),
            pltpu.VMEM((2, C * CHUNK, LANES), F32),
            pltpu.VMEM((C * 2 * TAIL, LANES), F32),
        ],
        compiler_params=pltpu.CompilerParams(vmem_limit_bytes=40 * MIB),
        cost_estimate=pl.CostEstimate(flops=2 * ROWS * COLS * C * 4 * C, bytes_accessed=10 * MIB, transcendentals=0),
        name="edges",
    )(pair, gain[None, :], bias[None, :], weight)


def regroup(pieces, lane):
    out = []
    for b in range(PACK):
        total = None
        for a in range(PACK):
            shift = ((a - b) * REST) % LANES
            moved = pltpu.roll(pieces[a], shift, 1) if shift else pieces[a]
            total = moved if total is None else jnp.where(lane // REST == a, moved, total)
        out.append(total)
    return out


def triangle_kernel(
    edges_ref, out_ref, left, right, right_t, rest, rest_left, rest_right, tri, tri_rest, packed, sems
):
    loads = []
    for r in range(N_ROW):
        for c in range(N_CHAN):
            s = r * N_CHAN + c
            for side, dst in ((1, right), (0, left)):
                loads.append(
                    pltpu.make_async_copy(
                        edges_ref.at[s, pl.ds(side * COLS, COLS), :],
                        dst.at[pl.ds(c * COLS, COLS), pl.ds(r * LANES, LANES)],
                        sems.at[side],
                    )
                )
    tails = pltpu.make_async_copy(edges_ref.at[:, pl.ds(2 * COLS, 2 * TAIL), :], rest, sems.at[2])
    tails.start()
    for load in loads:
        load.start()
    tails.wait()
    lane = lax.broadcasted_iota(jnp.int32, (2 * TAIL, LANES), 1)

    @pl.loop(0, N_CHAN)
    def _(c):
        for q in range(N_ROW // PACK):
            pieces = [rest[(q * PACK + a) * N_CHAN + c].astype(F32) for a in range(PACK)]
            for b, value in enumerate(regroup(pieces, lane)):
                rest_left[q, pl.ds(c * COLS + b, TAIL, stride=PACK), :] = value[:TAIL]
                rest_right[q, pl.ds(c * COLS + b, TAIL, stride=PACK), :] = value[TAIL:]

    for load in loads:
        load.wait()
    for q in range(N_ROW // PACK):
        left[:, (N_ROW + q) * LANES : (N_ROW + q + 1) * LANES] = rest_left[q].astype(BF16)
    for r in range(N_ROW):
        right_t[r * ROWS : r * ROWS + LANES, :] = right[:, r * LANES : (r + 1) * LANES].T
    for q in range(N_ROW // PACK):
        turned = rest_right[q].astype(BF16).T
        for a in range(PACK):
            at = (q * PACK + a) * ROWS + LANES
            right_t[at : at + REST, :] = turned[a * REST : (a + 1) * REST]

    stores = []
    width = 256
    for n in range(SIDE // width):
        part = jnp.dot(right_t[...], left[:, n * width : (n + 1) * width], preferred_element_type=F32)
        if n < SIDE // width - 1:
            tri[:, n * width : (n + 1) * width] = part.astype(BF16)
            for r in (2 * n, 2 * n + 1):
                for c in range(N_CHAN):
                    store = pltpu.make_async_copy(
                        tri.at[pl.ds(c * COLS, COLS), pl.ds(r * LANES, LANES)],
                        out_ref.at[r * N_CHAN + c, pl.ds(0, COLS), :],
                        sems.at[3],
                    )
                    store.start()
                    stores.append(store)
        else:
            for q in range(N_ROW // PACK):
                tri_rest[q] = part[:, q * LANES : (q + 1) * LANES]

    lane = lax.broadcasted_iota(jnp.int32, (TAIL, LANES), 1)

    @pl.loop(0, N_CHAN)
    def _(c):
        for q in range(N_ROW // PACK):
            pieces = [
                tri_rest[q, pl.ds(c * COLS + b, TAIL, stride=PACK), :] for b in range(PACK)
            ]
            for a, value in enumerate(regroup(pieces, lane)):
                value = jnp.concatenate([value, jnp.zeros((BACK - COLS - TAIL, LANES), F32)], axis=0)
                packed[(q * PACK + a) * N_CHAN + c] = value.astype(BF16)

    store = pltpu.make_async_copy(packed, out_ref.at[:, pl.ds(COLS, BACK - COLS), :], sems.at[4])
    store.start()
    store.wait()
    for store in stores:
        store.wait()


def triangle(edges_all):
    return pl.pallas_call(
        triangle_kernel,
        in_specs=[pl.BlockSpec(memory_space=pl.ANY)],
        out_specs=pl.BlockSpec(memory_space=pl.ANY),
        out_shape=jax.ShapeDtypeStruct((N_ROW * N_CHAN, BACK, LANES), BF16),
        scratch_shapes=[
            pltpu.VMEM((SIDE, SIDE), BF16),
            pltpu.VMEM((SIDE, N_ROW * LANES), BF16),
            pltpu.VMEM((SIDE, SIDE), BF16),
            pltpu.VMEM((N_ROW * N_CHAN, 2 * TAIL, LANES), BF16),
            pltpu.VMEM((N_ROW // PACK, SIDE, LANES), F32),
            pltpu.VMEM((N_ROW // PACK, SIDE, LANES), F32),
            pltpu.VMEM((SIDE, N_ROW * LANES), BF16),
            pltpu.VMEM((N_ROW // PACK, SIDE, LANES), F32),
            pltpu.VMEM((N_ROW * N_CHAN, BACK - COLS, LANES), BF16),
            pltpu.SemaphoreType.DMA((5,)),
        ],
        compiler_params=pltpu.CompilerParams(vmem_limit_bytes=48 * MIB),
        cost_estimate=pl.CostEstimate(flops=2 * SIDE**3, bytes_accessed=10 * MIB, transcendentals=0),
        name="triangle",
    )(edges_all)


def finish_kernel(tri_ref, gate_ref, gain_ref, bias_ref, weight_ref, out_ref, wide, dense, tail):
    step = pl.program_id(0)
    full = COLS // CHUNK
    gain, bias, weight = gain_ref[...], bias_ref[...], weight_ref[...]

    @pl.loop(0, C // 8)
    def _(n):
        at = pl.multiple_of(n * 8 * CHUNK, 8 * CHUNK)
        wide[pl.ds(at, 8 * CHUNK), :] = tri_ref[pl.ds(8 * n, 8)].reshape(8 * CHUNK, LANES).astype(F32)

    def project(g):
        normed = layer_norm(wide[pl.ds(g, C, stride=CHUNK), :], gain, bias, 0).astype(BF16)
        return lax.dot_general(normed, weight, (((0,), (0,)), ((), ())), preferred_element_type=F32)

    @pl.when(step < full)
    def _():
        @pl.loop(0, CHUNK)
        def _(g):
            dense[pl.ds(g, LANES, stride=CHUNK), :] = project(g)

        to = pl.multiple_of(step * CHUNK, CHUNK)

        @pl.loop(0, LANES // 8)
        def _(n):
            at = pl.multiple_of(n * 8 * CHUNK, 8 * CHUNK)
            value = dense[pl.ds(at, 8 * CHUNK), :].reshape(8, CHUNK, C)
            gate = gate_ref[pl.ds(8 * n, 8), pl.ds(to, CHUNK), :].astype(F32)
            out_ref[pl.ds(8 * n, 8), pl.ds(to, CHUNK), :] = (gate * value).astype(BF16)

    @pl.when(step >= full)
    def _():
        first = (step - full) * CHUNK

        @pl.loop(0, jnp.minimum(CHUNK, TAIL - first))
        def _(g):
            value = project(g)
            for e in range(PACK):
                tail[pl.ds(PACK * (first + g) + e, REST, stride=COLS), :] = value[e * REST : (e + 1) * REST]

    @pl.when(step == pl.num_programs(0) - 1)
    def _():
        @pl.loop(0, REST // 8)
        def _(n):
            at = pl.multiple_of(n * 8 * COLS, 8 * COLS)
            value = tail[pl.ds(at, 8 * COLS), :].reshape(8, COLS, C)
            gate = gate_ref[pl.ds(LANES + 8 * n, 8)].astype(F32)
            out_ref[pl.ds(LANES + 8 * n, 8)] = (gate * value).astype(BF16)


def finish(tri, gate, gain, bias, weight):
    steps = COLS // CHUNK + -(-TAIL // CHUNK)
    return pl.pallas_call(
        finish_kernel,
        grid=(steps,),
        in_specs=[
            pl.BlockSpec((C, CHUNK, LANES), lambda t: (0, t, 0)),
            pl.BlockSpec((ROWS, COLS, C), lambda t: (0, 0, 0)),
            pl.BlockSpec((C, 1), lambda t: (0, 0)),
            pl.BlockSpec((C, 1), lambda t: (0, 0)),
            pl.BlockSpec((C, C), lambda t: (0, 0)),
        ],
        out_specs=pl.BlockSpec((ROWS, COLS, C), lambda t: (0, 0, 0)),
        out_shape=jax.ShapeDtypeStruct((ROWS, COLS, C), BF16),
        scratch_shapes=[
            pltpu.VMEM((C * CHUNK, LANES), F32),
            pltpu.VMEM((LANES * CHUNK, C), F32),
            pltpu.VMEM((REST * COLS, C), F32),
        ],
        compiler_params=pltpu.CompilerParams(vmem_limit_bytes=40 * MIB),
        cost_estimate=pl.CostEstimate(flops=2 * ROWS * COLS * C * C, bytes_accessed=10 * MIB, transcendentals=0),
        name="finish",
    )(tri, gate, gain[:, None], bias[:, None], weight)


def shards(pair, in_gain, in_bias, edge_weight, gate_weight, out_gain, out_bias, out_weight):
    both = edges(pair, in_gain, in_bias, edge_weight)
    both_all = lax.all_to_all(both, ("row", "chan"), split_axis=0, concat_axis=0, tiled=True)
    normed = layer_norm(pair.astype(F32), in_gain, in_bias, -1).astype(BF16)
    gate = jax.nn.sigmoid(
        jnp.einsum("pqc,cd->pqd", normed, gate_weight, preferred_element_type=F32)
    ).astype(BF16)
    tri = lax.all_to_all(triangle(both_all), ("row", "chan"), split_axis=0, concat_axis=0, tiled=True)
    return finish(tri, gate, out_gain, out_bias, out_weight)


def solution(mesh):
    return jax.shard_map(
        shards,
        mesh=mesh,
        in_specs=(P("row", "chan", None), P(), P(), P(), P(), P(), P(), P()),
        out_specs=P("row", "chan", None),
        check_vma=False,
    )
```

```python
import jax
import jax.numpy as jnp
from jax import lax
from jax.experimental import pallas as pl
from jax.experimental.pallas import tpu as pltpu
from jax.sharding import PartitionSpec as P

ROWS, COLS, C = 160, 80, 128
LANES = 128
REST = ROWS - LANES
PACK = LANES // REST
TAIL = COLS // PACK
CHUNK = 16
CHUNKS = COLS // CHUNK
BOTH = 2 * (COLS + TAIL)
BACK = 104
N_ROW, N_CHAN = 8, 16
SIDE = 1280
F32, BF16 = jnp.float32, jnp.bfloat16
MIB = 1 << 20
VMEM_BYTES = 60 * MIB


def sigmoid(x):
    return 0.5 * jnp.tanh(0.5 * x) + 0.5


def layer_norm(values, gain, bias, axis):
    mean = jnp.mean(values, axis=axis, keepdims=True)
    centred = values - mean
    var = jnp.mean(centred * centred, axis=axis, keepdims=True)
    return centred * lax.rsqrt(var + 1e-05) * gain + bias


def edges_kernel(pair_ref, gain_ref, bias_ref, weight_ref, out_ref, weight_t, held, normed, dense, tail, done, sems):
    loads = [
        pltpu.make_async_copy(pair_ref.at[:, pl.ds(t * CHUNK, CHUNK), :], held.at[t], sems.at[t]) for t in range(CHUNKS)
    ]
    for load in loads:
        load.start()
    for m in range(4):
        weight_t[m * 128 : (m + 1) * 128, :] = weight_ref[:, m * 128 : (m + 1) * 128].T
    gain, bias = gain_ref[...], bias_ref[...]

    def product(x, side):
        both = lax.dot_general(
            weight_t[side * 256 : (side + 1) * 256, :], x, (((1,), (1,)), ((), ())), preferred_element_type=F32
        )
        return sigmoid(both[128:]) * both[:128]

    def store(t, side):
        rows = pl.ds(pl.multiple_of(side * COLS + t * CHUNK, CHUNK), CHUNK)
        return pltpu.make_async_copy(done.at[:, rows, :], out_ref.at[:, rows, :], sems.at[CHUNKS + side])

    @pl.loop(0, CHUNKS)
    def _(t):
        pltpu.make_async_copy(pair_ref.at[:, pl.ds(t * CHUNK, CHUNK), :], held.at[t], sems.at[t]).wait()
        group = 8
        for n in range(ROWS // group):
            block = held[t, n * group : (n + 1) * group].reshape(group * CHUNK, C).astype(F32)
            normed[n * group * CHUNK : (n + 1) * group * CHUNK, :] = layer_norm(block, gain, bias, -1)
        for n in range(CHUNK // 2):
            x = jnp.concatenate(
                [normed[pl.ds(2 * n + e, LANES, stride=CHUNK), :] for e in range(2)], axis=0
            ).astype(BF16)
            for side in range(2):
                value = product(x, side)
                for e in range(2):
                    dense[side, pl.ds(2 * n + e, C, stride=CHUNK), :] = value[:, e * 128 : (e + 1) * 128]
        for n in range(CHUNK // 8):
            x = jnp.concatenate(
                [normed[pl.ds(LANES * CHUNK + 8 * n + e, REST, stride=CHUNK), :] for e in range(8)], axis=0
            ).astype(BF16)
            for side in range(2):
                value = product(x, side)
                for e in range(2):
                    at = side * TAIL + 4 * t + 2 * n + e
                    tail[pl.ds(at, C, stride=2 * TAIL), :] = value[:, e * 128 : (e + 1) * 128]
        for side in range(2):
            to = pl.multiple_of(side * COLS + t * CHUNK, CHUNK)
            for n in range(C // 8):
                done[8 * n : 8 * n + 8, pl.ds(to, CHUNK), :] = (
                    dense[side, n * 8 * CHUNK : (n + 1) * 8 * CHUNK, :].reshape(8, CHUNK, LANES).astype(BF16)
                )
            store(t, side).start()

    for n in range(C // 8):
        done[8 * n : 8 * n + 8, 2 * COLS :, :] = (
            tail[n * 16 * TAIL : (n + 1) * 16 * TAIL, :].reshape(8, 2 * TAIL, LANES).astype(BF16)
        )
    rows = pl.ds(2 * COLS, 2 * TAIL)
    last = pltpu.make_async_copy(done.at[:, rows, :], out_ref.at[:, rows, :], sems.at[CHUNKS + 2])
    last.start()
    last.wait()
    for t in range(CHUNKS):
        for side in range(2):
            store(t, side).wait()


def edges(pair, gain, bias, weight):
    vmem = pl.BlockSpec(memory_space=pltpu.VMEM)
    return pl.pallas_call(
        edges_kernel,
        in_specs=[pl.BlockSpec(memory_space=pl.ANY), vmem, vmem, vmem],
        out_specs=pl.BlockSpec(memory_space=pl.ANY),
        out_shape=jax.ShapeDtypeStruct((C, BOTH, LANES), BF16),
        scratch_shapes=[
            pltpu.VMEM((4 * C, C), BF16),
            pltpu.VMEM((CHUNKS, ROWS, CHUNK, C), BF16),
            pltpu.VMEM((ROWS * CHUNK, C), F32),
            pltpu.VMEM((2, C * CHUNK, LANES), F32),
            pltpu.VMEM((C * 2 * TAIL, LANES), F32),
            pltpu.VMEM((C, BOTH, LANES), BF16),
            pltpu.SemaphoreType.DMA((CHUNKS + 3,)),
        ],
        compiler_params=pltpu.CompilerParams(vmem_limit_bytes=VMEM_BYTES),
        cost_estimate=pl.CostEstimate(flops=2 * ROWS * COLS * C * 4 * C, bytes_accessed=10 * MIB, transcendentals=0),
        name="edges",
    )(pair, gain[None, :], bias[None, :], weight)


def regroup(pieces, lane):
    out = []
    for b in range(PACK):
        total = None
        for a in range(PACK):
            shift = ((a - b) * REST) % LANES
            moved = pltpu.roll(pieces[a], shift, 1) if shift else pieces[a]
            total = moved if total is None else jnp.where(lane // REST == a, moved, total)
        out.append(total)
    return out


def triangle_kernel(
    edges_ref, out_ref, left, right, right_t, rest, rest_left, rest_right, tri, tri_rest, packed, sems
):
    loads = []
    for r in range(N_ROW):
        for c in range(N_CHAN):
            s = r * N_CHAN + c
            for side, dst in ((1, right), (0, left)):
                loads.append(
                    pltpu.make_async_copy(
                        edges_ref.at[s, pl.ds(side * COLS, COLS), :],
                        dst.at[pl.ds(c * COLS, COLS), pl.ds(r * LANES, LANES)],
                        sems.at[side],
                    )
                )
    tails = pltpu.make_async_copy(edges_ref.at[:, pl.ds(2 * COLS, 2 * TAIL), :], rest, sems.at[2])
    tails.start()
    for load in loads:
        load.start()
    tails.wait()
    lane = lax.broadcasted_iota(jnp.int32, (2 * TAIL, LANES), 1)

    @pl.loop(0, N_CHAN)
    def _(c):
        for q in range(N_ROW // PACK):
            pieces = [rest[(q * PACK + a) * N_CHAN + c].astype(F32) for a in range(PACK)]
            for b, value in enumerate(regroup(pieces, lane)):
                rest_left[q, pl.ds(c * COLS + b, TAIL, stride=PACK), :] = value[:TAIL]
                rest_right[q, pl.ds(c * COLS + b, TAIL, stride=PACK), :] = value[TAIL:]

    for load in loads:
        load.wait()
    for q in range(N_ROW // PACK):
        left[:, (N_ROW + q) * LANES : (N_ROW + q + 1) * LANES] = rest_left[q].astype(BF16)
    for r in range(N_ROW):
        right_t[r * ROWS : r * ROWS + LANES, :] = right[:, r * LANES : (r + 1) * LANES].T
    for q in range(N_ROW // PACK):
        turned = rest_right[q].astype(BF16).T
        for a in range(PACK):
            at = (q * PACK + a) * ROWS + LANES
            right_t[at : at + REST, :] = turned[a * REST : (a + 1) * REST]

    stores = []
    width = 256
    for n in range(SIDE // width):
        part = jnp.dot(right_t[...], left[:, n * width : (n + 1) * width], preferred_element_type=F32)
        if n < SIDE // width - 1:
            tri[:, n * width : (n + 1) * width] = part.astype(BF16)
            for r in (2 * n, 2 * n + 1):
                for c in range(N_CHAN):
                    store = pltpu.make_async_copy(
                        tri.at[pl.ds(c * COLS, COLS), pl.ds(r * LANES, LANES)],
                        out_ref.at[r * N_CHAN + c, pl.ds(0, COLS), :],
                        sems.at[3],
                    )
                    store.start()
                    stores.append(store)
        else:
            for q in range(N_ROW // PACK):
                tri_rest[q] = part[:, q * LANES : (q + 1) * LANES]

    lane = lax.broadcasted_iota(jnp.int32, (TAIL, LANES), 1)

    @pl.loop(0, N_CHAN)
    def _(c):
        for q in range(N_ROW // PACK):
            pieces = [
                tri_rest[q, pl.ds(c * COLS + b, TAIL, stride=PACK), :] for b in range(PACK)
            ]
            for a, value in enumerate(regroup(pieces, lane)):
                value = jnp.concatenate([value, jnp.zeros((BACK - COLS - TAIL, LANES), F32)], axis=0)
                packed[(q * PACK + a) * N_CHAN + c] = value.astype(BF16)

    store = pltpu.make_async_copy(packed, out_ref.at[:, pl.ds(COLS, BACK - COLS), :], sems.at[4])
    store.start()
    store.wait()
    for store in stores:
        store.wait()


def triangle(edges_all):
    return pl.pallas_call(
        triangle_kernel,
        in_specs=[pl.BlockSpec(memory_space=pl.ANY)],
        out_specs=pl.BlockSpec(memory_space=pl.ANY),
        out_shape=jax.ShapeDtypeStruct((N_ROW * N_CHAN, BACK, LANES), BF16),
        scratch_shapes=[
            pltpu.VMEM((SIDE, SIDE), BF16),
            pltpu.VMEM((SIDE, N_ROW * LANES), BF16),
            pltpu.VMEM((SIDE, SIDE), BF16),
            pltpu.VMEM((N_ROW * N_CHAN, 2 * TAIL, LANES), BF16),
            pltpu.VMEM((N_ROW // PACK, SIDE, LANES), F32),
            pltpu.VMEM((N_ROW // PACK, SIDE, LANES), F32),
            pltpu.VMEM((SIDE, N_ROW * LANES), BF16),
            pltpu.VMEM((N_ROW // PACK, SIDE, LANES), F32),
            pltpu.VMEM((N_ROW * N_CHAN, BACK - COLS, LANES), BF16),
            pltpu.SemaphoreType.DMA((5,)),
        ],
        compiler_params=pltpu.CompilerParams(vmem_limit_bytes=VMEM_BYTES),
        cost_estimate=pl.CostEstimate(flops=2 * SIDE**3, bytes_accessed=10 * MIB, transcendentals=0),
        name="triangle",
    )(edges_all)


def finish_kernel(
    tri_ref, gate_ref, gain_ref, bias_ref, weight_ref, out_ref, held, held_gate, wide, dense, tail, done, sems
):
    span = BACK - COLS

    def load(t):
        rows = pl.ds(pl.multiple_of(t * CHUNK, CHUNK), CHUNK)
        return (
            pltpu.make_async_copy(tri_ref.at[:, rows, :], held.at[:, rows, :], sems.at[t]),
            pltpu.make_async_copy(
                gate_ref.at[pl.ds(0, LANES), rows, :], held_gate.at[pl.ds(0, LANES), rows, :], sems.at[CHUNKS + t]
            ),
        )

    def store(t):
        rows = pl.ds(pl.multiple_of(t * CHUNK, CHUNK), CHUNK)
        return pltpu.make_async_copy(
            done.at[pl.ds(0, LANES), rows, :], out_ref.at[pl.ds(0, LANES), rows, :], sems.at[2 * CHUNKS + 2]
        )

    rows, rest = pl.ds(COLS, span), pl.ds(LANES, REST)
    tri_tail = pltpu.make_async_copy(tri_ref.at[:, rows, :], held.at[:, rows, :], sems.at[2 * CHUNKS])
    gate_tail = pltpu.make_async_copy(gate_ref.at[rest], held_gate.at[rest], sems.at[2 * CHUNKS + 1])
    tri_tail.start()
    for t in range(CHUNKS):
        for copy in load(t):
            copy.start()
    gate_tail.start()
    gain = jnp.broadcast_to(gain_ref[...], (LANES, C)).T
    bias = jnp.broadcast_to(bias_ref[...], (LANES, C)).T
    weight = weight_ref[...]

    def project(g, stride):
        normed = layer_norm(wide[pl.ds(g, C, stride=stride), :], gain, bias, 0).astype(BF16)
        return lax.dot_general(normed, weight, (((0,), (0,)), ((), ())), preferred_element_type=F32)

    tri_tail.wait()
    for n in range(C // 8):
        wide[n * 8 * span : (n + 1) * 8 * span, :] = held[8 * n : 8 * n + 8, COLS:, :].reshape(8 * span, LANES).astype(F32)
    for m in range(TAIL):
        value = project(m, span)
        for e in range(PACK):
            tail[pl.ds(PACK * m + e, REST, stride=COLS), :] = value[e * REST : (e + 1) * REST]

    @pl.loop(0, CHUNKS)
    def _(t):
        for copy in load(t):
            copy.wait()
        to = pl.multiple_of(t * CHUNK, CHUNK)
        for n in range(C // 8):
            wide[n * 8 * CHUNK : (n + 1) * 8 * CHUNK, :] = (
                held[8 * n : 8 * n + 8, pl.ds(to, CHUNK), :].reshape(8 * CHUNK, LANES).astype(F32)
            )
        for g in range(CHUNK):
            dense[pl.ds(g, LANES, stride=CHUNK), :] = project(g, CHUNK)
        for n in range(LANES // 8):
            value = dense[n * 8 * CHUNK : (n + 1) * 8 * CHUNK, :].reshape(8, CHUNK, C)
            gate = held_gate[8 * n : 8 * n + 8, pl.ds(to, CHUNK), :].astype(F32)
            done[8 * n : 8 * n + 8, pl.ds(to, CHUNK), :] = (gate * value).astype(BF16)
        store(t).start()

    gate_tail.wait()
    for n in range(REST // 8):
        value = tail[n * 8 * COLS : (n + 1) * 8 * COLS, :].reshape(8, COLS, C)
        gate = held_gate[LANES + 8 * n : LANES + 8 * n + 8].astype(F32)
        done[LANES + 8 * n : LANES + 8 * n + 8] = (gate * value).astype(BF16)
    last = pltpu.make_async_copy(done.at[rest], out_ref.at[rest], sems.at[2 * CHUNKS + 3])
    last.start()
    last.wait()
    for t in range(CHUNKS):
        store(t).wait()


def finish(tri, gate, gain, bias, weight):
    vmem, hbm = pl.BlockSpec(memory_space=pltpu.VMEM), pl.BlockSpec(memory_space=pl.ANY)
    return pl.pallas_call(
        finish_kernel,
        in_specs=[hbm, hbm, vmem, vmem, vmem],
        out_specs=hbm,
        out_shape=jax.ShapeDtypeStruct((ROWS, COLS, C), BF16),
        scratch_shapes=[
            pltpu.VMEM((C, BACK, LANES), BF16),
            pltpu.VMEM((ROWS, COLS, C), BF16),
            pltpu.VMEM((C * (BACK - COLS), LANES), F32),
            pltpu.VMEM((LANES * CHUNK, C), F32),
            pltpu.VMEM((REST * COLS, C), F32),
            pltpu.VMEM((ROWS, COLS, C), BF16),
            pltpu.SemaphoreType.DMA((2 * CHUNKS + 4,)),
        ],
        compiler_params=pltpu.CompilerParams(vmem_limit_bytes=VMEM_BYTES),
        cost_estimate=pl.CostEstimate(flops=2 * ROWS * COLS * C * C, bytes_accessed=10 * MIB, transcendentals=0),
        name="finish",
    )(tri, gate, gain[None, :], bias[None, :], weight)


def shards(pair, in_gain, in_bias, edge_weight, gate_weight, out_gain, out_bias, out_weight):
    both = edges(pair, in_gain, in_bias, edge_weight)
    both_all = lax.all_to_all(both, ("row", "chan"), split_axis=0, concat_axis=0, tiled=True)
    normed = layer_norm(pair.astype(F32), in_gain, in_bias, -1).astype(BF16)
    gate = jax.nn.sigmoid(
        jnp.einsum("pqc,cd->pqd", normed, gate_weight, preferred_element_type=F32)
    ).astype(BF16)
    tri = lax.all_to_all(triangle(both_all), ("row", "chan"), split_axis=0, concat_axis=0, tiled=True)
    return finish(tri, gate, out_gain, out_bias, out_weight)


def solution(mesh):
    return jax.shard_map(
        shards,
        mesh=mesh,
        in_specs=(P("row", "chan", None), P(), P(), P(), P(), P(), P(), P()),
        out_specs=P("row", "chan", None),
        check_vma=False,
    )
```

```python
import jax
import jax.numpy as jnp
from jax import lax
from jax.experimental import pallas as pl
from jax.experimental.pallas import tpu as pltpu
from jax.sharding import Mesh, PartitionSpec as P

ROWS, COLS, C = 160, 80, 128
LANES = 128
REST = ROWS - LANES
PACK = LANES // REST
TAIL = COLS // PACK
CHUNK = 16
CHUNKS = COLS // CHUNK
STEP = CHUNK + 4
TAIL_STEP = 2 * TAIL + 4
COLS_STEP = COLS + 4
BOTH = 2 * (COLS + TAIL)
BACK = 104
N_ROW, N_CHAN = 8, 16
SIZES = {"y": 4, "z_lo": 2, "core": 2, "z_hi": 2, "x": 4}
ROW, CHAN = ("z_hi", "x"), ("y", "z_lo", "core")
OUT_ORDER = ROW + CHAN
BACK_ORDER = ("y", "x", "core", "z_lo", "z_hi")
SIDE = 1280
F32, BF16 = jnp.float32, jnp.bfloat16
MIB = 1 << 20
VMEM_BYTES = 36 * MIB


def places(order, inside):
    found = []
    for n in range(N_ROW * N_CHAN):
        at = {}
        for axis in reversed(inside):
            n, at[axis] = divmod(n, SIZES[axis])
        number = 0
        for axis in order:
            number = number * SIZES[axis] + at[axis]
        found.append(number)
    return found


OUT_OF_CHANNEL = places(OUT_ORDER, BACK_ORDER)
FROM_BLOCK = places(OUT_ORDER, ROW + CHAN)
BACK_TO_BLOCK = places(BACK_ORDER, ROW + CHAN)


def layer_norm(values, gain, bias, axis):
    mean = jnp.mean(values, axis=axis, keepdims=True)
    centred = values - mean
    var = jnp.mean(centred * centred, axis=axis, keepdims=True)
    return centred * lax.rsqrt(var + 1e-05) * gain + bias


def fetch(sources, targets, sems):
    copies = [pltpu.make_async_copy(src, dst, sems.at[n]) for n, (src, dst) in enumerate(zip(sources, targets))]
    for copy in copies:
        copy.start()
    return copies


def edges_kernel(
    pair_ref, gain_hbm, bias_hbm, weight_hbm, out_ref, gain_ref, bias_ref, weight_ref, weight_t, held, normed, dense,
    tail, sems, small_sems
):
    loads = [
        pltpu.make_async_copy(pair_ref.at[:, pl.ds(t * CHUNK, CHUNK), :], held.at[t], sems.at[t]) for t in range(CHUNKS)
    ]
    for load in loads:
        load.start()
    small = (gain_ref, bias_ref, weight_ref)
    for copy in fetch((gain_hbm, bias_hbm, weight_hbm), small, small_sems):
        copy.wait()
    for m in range(4):
        turned = (0.5 * weight_ref[:, m * C : (m + 1) * C].astype(F32)).T.astype(BF16)
        for b in range(C // 16):
            at = 2 * C * (m // 2) + 32 * b + 16 * (m % 2)
            weight_t[at : at + 16, :] = turned[16 * b : 16 * b + 16]
    gain, bias = gain_ref[...], bias_ref[...]

    def product(x, side):
        both = lax.dot_general(
            weight_t[side * 2 * C : (side + 1) * 2 * C, :], x, (((1,), (1,)), ((), ())), preferred_element_type=F32
        )
        both = both.reshape(C // 16, 2, 16, x.shape[0])
        return (both[:, 0] * jnp.tanh(both[:, 1]) + both[:, 0]).reshape(C, x.shape[0])

    @pl.loop(0, CHUNKS)
    def _(t):
        pltpu.make_async_copy(pair_ref.at[:, pl.ds(t * CHUNK, CHUNK), :], held.at[t], sems.at[t]).wait()
        group = 8
        for n in range(ROWS // group):
            block = held[t, n * group : (n + 1) * group].reshape(group * CHUNK, C).astype(F32)
            block = layer_norm(block, gain, bias, -1)
            for u in range(group):
                at = (n * group + u) * STEP
                normed[at : at + CHUNK, :] = block[u * CHUNK : (u + 1) * CHUNK]
        for n in range(CHUNK // 2):
            x = jnp.concatenate(
                [normed[pl.ds(2 * n + e, LANES, stride=STEP), :] for e in range(2)], axis=0
            ).astype(BF16)
            for side in range(2):
                value = product(x, side)
                for e in range(2):
                    dense[side, pl.ds(2 * n + e, C, stride=STEP), :] = value[:, e * 128 : (e + 1) * 128]
        for n in range(CHUNK // 8):
            x = jnp.concatenate(
                [normed[pl.ds(LANES * STEP + 8 * n + e, REST, stride=STEP), :] for e in range(8)], axis=0
            ).astype(BF16)
            for side in range(2):
                value = product(x, side)
                for e in range(2):
                    at = side * TAIL + 4 * t + 2 * n + e
                    tail[pl.ds(at, C, stride=TAIL_STEP), :] = value[:, e * 128 : (e + 1) * 128]
        for side in range(2):
            to = pl.multiple_of(side * COLS + t * CHUNK, CHUNK)
            for h in range(C):
                out_ref[OUT_OF_CHANNEL[h], pl.ds(to, CHUNK), :] = dense[side, h * STEP : h * STEP + CHUNK, :].astype(BF16)

    for h in range(C):
        out_ref[OUT_OF_CHANNEL[h], 2 * COLS :, :] = tail[h * TAIL_STEP : h * TAIL_STEP + 2 * TAIL, :].astype(BF16)


def edges(pair, gain, bias, weight):
    vmem, hbm = pl.BlockSpec(memory_space=pltpu.VMEM), pl.BlockSpec(memory_space=pltpu.HBM)
    return pl.pallas_call(
        edges_kernel,
        in_specs=[hbm] * 4,
        out_specs=vmem,
        out_shape=jax.ShapeDtypeStruct((C, BOTH, LANES), BF16),
        scratch_shapes=[
            pltpu.VMEM((1, C), F32),
            pltpu.VMEM((1, C), F32),
            pltpu.VMEM((C, 4 * C), BF16),
            pltpu.VMEM((4 * C, C), BF16),
            pltpu.VMEM((CHUNKS, ROWS, CHUNK, C), BF16),
            pltpu.VMEM((ROWS * STEP, C), F32),
            pltpu.VMEM((2, C * STEP, LANES), F32),
            pltpu.VMEM((C * TAIL_STEP, LANES), F32),
            pltpu.SemaphoreType.DMA((CHUNKS,)),
            pltpu.SemaphoreType.DMA((3,)),
        ],
        compiler_params=pltpu.CompilerParams(vmem_limit_bytes=VMEM_BYTES),
        cost_estimate=pl.CostEstimate(flops=2 * ROWS * COLS * C * 4 * C, bytes_accessed=10 * MIB, transcendentals=0),
        name="edges",
    )(pair, gain[None, :], bias[None, :], weight)


def gate_kernel(
    pair_ref, gain_hbm, bias_hbm, weight_hbm, out_ref, gain_ref, bias_ref, weight_ref, held, sems
):
    for copy in fetch((pair_ref, gain_hbm, bias_hbm, weight_hbm), (held, gain_ref, bias_ref, weight_ref), sems):
        copy.wait()
    gain, bias, weight = gain_ref[...], bias_ref[...], weight_ref[...]
    group = 4

    @pl.loop(0, ROWS // group, unroll=2)
    def _(n):
        block = held[pl.ds(n * group, group)].reshape(group * COLS, C).astype(F32)
        normed = layer_norm(block, gain, bias, -1).astype(BF16)
        value = jax.nn.sigmoid(jnp.dot(normed, weight, preferred_element_type=F32))
        out_ref[pl.ds(n * group, group)] = value.astype(BF16).reshape(group, COLS, C)


def gates(pair, gain, bias, weight):
    vmem, hbm = pl.BlockSpec(memory_space=pltpu.VMEM), pl.BlockSpec(memory_space=pltpu.HBM)
    return pl.pallas_call(
        gate_kernel,
        in_specs=[hbm] * 4,
        out_specs=vmem,
        out_shape=jax.ShapeDtypeStruct((ROWS, COLS, C), BF16),
        scratch_shapes=[
            pltpu.VMEM((1, C), F32),
            pltpu.VMEM((1, C), F32),
            pltpu.VMEM((C, C), BF16),
            pltpu.VMEM((ROWS, COLS, C), BF16),
            pltpu.SemaphoreType.DMA((4,)),
        ],
        compiler_params=pltpu.CompilerParams(vmem_limit_bytes=VMEM_BYTES),
        cost_estimate=pl.CostEstimate(flops=2 * ROWS * COLS * C * C, bytes_accessed=30 * MIB, transcendentals=0),
        name="gates",
    )(pair, gain[None, :], bias[None, :], weight)


def regroup(pieces, lane):
    out = []
    for b in range(PACK):
        total = None
        for a in range(PACK):
            shift = ((a - b) * REST) % LANES
            moved = pltpu.roll(pieces[a], shift, 1) if shift else pieces[a]
            total = moved if total is None else jnp.where(lane // REST == a, moved, total)
        out.append(total)
    return out


def triangle_kernel(edges_ref, out_ref, left_rest, right_t, rest_left, rest_right, tri_rest):
    lane = lax.broadcasted_iota(jnp.int32, (2 * TAIL, LANES), 1)
    for c in range(N_CHAN):
        for q in range(N_ROW // PACK):
            blocks = [FROM_BLOCK[(q * PACK + a) * N_CHAN + c] for a in range(PACK)]
            pieces = [edges_ref[block, 2 * COLS :, :].astype(F32) for block in blocks]
            for b, value in enumerate(regroup(pieces, lane)):
                rest_left[q, pl.ds(c * COLS + b, TAIL, stride=PACK), :] = value[:TAIL]
                rest_right[q, pl.ds(c * COLS + b, TAIL, stride=PACK), :] = value[TAIL:]

    def side(r, first):
        blocks = FROM_BLOCK[r * N_CHAN : (r + 1) * N_CHAN]
        return jnp.concatenate([edges_ref[block, first : first + COLS, :] for block in blocks], axis=0)

    for q in range(N_ROW // PACK):
        left_rest[:, q * LANES : (q + 1) * LANES] = rest_left[q].astype(BF16)
        turned = rest_right[q].astype(BF16).T
        for a in range(PACK):
            at = (q * PACK + a) * ROWS + LANES
            right_t[at : at + REST, :] = turned[a * REST : (a + 1) * REST]
    for r in range(N_ROW):
        right_t[r * ROWS : r * ROWS + LANES, :] = side(r, COLS).T

    part = jnp.dot(right_t[...], left_rest[...], preferred_element_type=F32)
    for q in range(N_ROW // PACK):
        tri_rest[q] = part[:, q * LANES : (q + 1) * LANES]
    lane = lax.broadcasted_iota(jnp.int32, (TAIL, LANES), 1)
    for n in range(N_ROW // 2):
        for c in range(4 * n, 4 * n + 4):
            for q in range(N_ROW // PACK):
                pieces = [tri_rest[q, pl.ds(c * COLS + b, TAIL, stride=PACK), :] for b in range(PACK)]
                for a, value in enumerate(regroup(pieces, lane)):
                    value = jnp.concatenate([value, jnp.zeros((BACK - COLS - TAIL, LANES), F32)], axis=0)
                    out_ref[BACK_TO_BLOCK[(q * PACK + a) * N_CHAN + c], COLS:, :] = value.astype(BF16)
        pair = jnp.concatenate([side(2 * n, 0), side(2 * n + 1, 0)], axis=1)
        part = jnp.dot(right_t[...], pair, preferred_element_type=F32).astype(BF16)
        for e in range(2):
            r = 2 * n + e
            for c in range(N_CHAN):
                out_ref[BACK_TO_BLOCK[r * N_CHAN + c], :COLS, :] = part[
                    c * COLS : (c + 1) * COLS, e * LANES : (e + 1) * LANES
                ]


def triangle(edges_all):
    vmem = pl.BlockSpec(memory_space=pltpu.VMEM)
    return pl.pallas_call(
        triangle_kernel,
        in_specs=[vmem],
        out_specs=vmem,
        out_shape=jax.ShapeDtypeStruct((N_ROW * N_CHAN, BACK, LANES), BF16),
        scratch_shapes=[
            pltpu.VMEM((SIDE, 2 * LANES), BF16),
            pltpu.VMEM((SIDE, SIDE), BF16),
            pltpu.VMEM((N_ROW // PACK, SIDE, LANES), F32),
            pltpu.VMEM((N_ROW // PACK, SIDE, LANES), F32),
            pltpu.VMEM((N_ROW // PACK, SIDE, LANES), F32),
        ],
        compiler_params=pltpu.CompilerParams(vmem_limit_bytes=VMEM_BYTES),
        cost_estimate=pl.CostEstimate(flops=2 * SIDE**3, bytes_accessed=10 * MIB, transcendentals=0),
        name="triangle",
    )(edges_all)


def finish_kernel(
    held, gate_ref, gain_hbm, bias_hbm, weight_hbm, out_ref, gain_ref, bias_ref, weight_ref, wide, dense, tail, done,
    sems, small_sems
):
    def store(t):
        rows = pl.ds(pl.multiple_of(t * CHUNK, CHUNK), CHUNK)
        return pltpu.make_async_copy(
            done.at[pl.ds(0, LANES), rows, :], out_ref.at[pl.ds(0, LANES), rows, :], sems.at[0]
        )

    rest = pl.ds(LANES, REST)
    small = (gain_ref, bias_ref, weight_ref)
    for copy in fetch((gain_hbm, bias_hbm, weight_hbm), small, small_sems):
        copy.wait()
    gain = jnp.broadcast_to(gain_ref[...], (LANES, C)).T
    bias = jnp.broadcast_to(bias_ref[...], (LANES, C)).T
    weight = weight_ref[...]

    def project(g):
        normed = layer_norm(wide[pl.ds(g, C, stride=STEP), :], gain, bias, 0).astype(BF16)
        return lax.dot_general(normed, weight, (((0,), (0,)), ((), ())), preferred_element_type=F32)

    for h in range(C):
        wide[h * STEP : h * STEP + TAIL, :] = held[h, COLS:, :].astype(F32)[:TAIL]
    for m in range(TAIL):
        value = project(m)
        for e in range(PACK):
            tail[pl.ds(PACK * m + e, REST, stride=COLS_STEP), :] = value[e * REST : (e + 1) * REST]

    @pl.loop(0, CHUNKS)
    def _(t):
        to = pl.multiple_of(t * CHUNK, CHUNK)
        for h in range(C):
            wide[h * STEP : h * STEP + CHUNK, :] = held[h, pl.ds(to, CHUNK), :].astype(F32)
        for g in range(CHUNK):
            dense[pl.ds(g, LANES, stride=STEP), :] = project(g)
        for i in range(LANES):
            gate = gate_ref[i, pl.ds(to, CHUNK), :].astype(F32)
            done[i, pl.ds(to, CHUNK), :] = (gate * dense[i * STEP : i * STEP + CHUNK, :]).astype(BF16)
        store(t).start()

    for i in range(REST):
        gate = gate_ref[LANES + i].astype(F32)
        done[LANES + i] = (gate * tail[i * COLS_STEP : i * COLS_STEP + COLS, :]).astype(BF16)
    last = pltpu.make_async_copy(done.at[rest], out_ref.at[rest], sems.at[1])
    last.start()
    last.wait()
    for t in range(CHUNKS):
        store(t).wait()


def finish(tri, gate, gain, bias, weight):
    vmem, hbm = pl.BlockSpec(memory_space=pltpu.VMEM), pl.BlockSpec(memory_space=pltpu.HBM)
    return pl.pallas_call(
        finish_kernel,
        in_specs=[vmem, vmem, hbm, hbm, hbm],
        out_specs=hbm,
        out_shape=jax.ShapeDtypeStruct((ROWS, COLS, C), BF16),
        scratch_shapes=[
            pltpu.VMEM((1, C), F32),
            pltpu.VMEM((1, C), F32),
            pltpu.VMEM((C, C), BF16),
            pltpu.VMEM((C * STEP, LANES), F32),
            pltpu.VMEM((LANES * STEP, C), F32),
            pltpu.VMEM((REST * COLS_STEP, C), F32),
            pltpu.VMEM((ROWS, COLS, C), BF16),
            pltpu.SemaphoreType.DMA((2,)),
            pltpu.SemaphoreType.DMA((3,)),
        ],
        compiler_params=pltpu.CompilerParams(vmem_limit_bytes=VMEM_BYTES),
        cost_estimate=pl.CostEstimate(flops=2 * ROWS * COLS * C * C, bytes_accessed=10 * MIB, transcendentals=0),
        name="finish",
    )(tri, gate, gain[None, :], bias[None, :], weight)


def shards(pair, in_gain, in_bias, edge_weight, gate_weight, out_gain, out_bias, out_weight):
    both = edges(pair, in_gain, in_bias, edge_weight)
    both_all = lax.all_to_all(both, OUT_ORDER, split_axis=0, concat_axis=0, tiled=True)
    gate = gates(pair, in_gain, in_bias, gate_weight)
    tri = lax.all_to_all(triangle(both_all), BACK_ORDER, split_axis=0, concat_axis=0, tiled=True)
    return finish(tri, gate, out_gain, out_bias, out_weight)


def solution(mesh):
    apart = Mesh(mesh.devices.reshape(tuple(SIZES.values())), tuple(SIZES))
    return jax.shard_map(
        shards,
        mesh=apart,
        in_specs=(P(ROW, CHAN, None), P(), P(), P(), P(), P(), P(), P()),
        out_specs=P(ROW, CHAN, None),
        check_vma=False,
    )
```

```python
import jax
import jax.numpy as jnp
from jax import lax
from jax.experimental import pallas as pl
from jax.experimental.pallas import tpu as pltpu
from jax.sharding import Mesh, PartitionSpec as P

ROWS, COLS, C = 160, 80, 128
LANES = 128
REST = ROWS - LANES
PACK = LANES // REST
TAIL = COLS // PACK
CHUNK = 16
CHUNKS = COLS // CHUNK
STEP = CHUNK + 4
TAIL_STEP = 2 * TAIL + 4
COLS_STEP = COLS + 4
BOTH = 2 * (COLS + TAIL)
BACK = 104
N_ROW, N_CHAN = 8, 16
SIZES = {"y": 4, "z_lo": 2, "core": 2, "z_hi": 2, "x": 4}
ROW, CHAN = ("z_hi", "x"), ("y", "z_lo", "core")
OUT_ORDER = ROW + CHAN
BACK_ORDER = ("y", "x", "core", "z_lo", "z_hi")
SIDE = 1280
F32, BF16 = jnp.float32, jnp.bfloat16
MIB = 1 << 20
VMEM_BYTES = 36 * MIB


def places(order, inside):
    found = []
    for n in range(N_ROW * N_CHAN):
        at = {}
        for axis in reversed(inside):
            n, at[axis] = divmod(n, SIZES[axis])
        number = 0
        for axis in order:
            number = number * SIZES[axis] + at[axis]
        found.append(number)
    return found


OUT_OF_CHANNEL = places(OUT_ORDER, BACK_ORDER)
FROM_BLOCK = places(OUT_ORDER, ROW + CHAN)
BACK_TO_BLOCK = places(BACK_ORDER, ROW + CHAN)


def layer_norm(values, gain, bias, axis):
    mean = jnp.mean(values, axis=axis, keepdims=True)
    centred = values - mean
    var = jnp.mean(centred * centred, axis=axis, keepdims=True)
    return centred * lax.rsqrt(var + 1e-05) * gain + bias


def in_hbm(*arrays):
    return [pltpu.with_memory_space_constraint(array, pltpu.HBM) for array in arrays]


def fetch(sources, targets, sems):
    copies = [pltpu.make_async_copy(src, dst, sems.at[n]) for n, (src, dst) in enumerate(zip(sources, targets))]
    for copy in copies:
        copy.start()
    return copies


def edges_kernel(
    pair_ref, gain_hbm, bias_hbm, weight_hbm, out_ref, gain_ref, bias_ref, weight_ref, weight_t, held, normed, dense,
    tail, sems, small_sems
):
    small = fetch((gain_hbm, bias_hbm, weight_hbm), (gain_ref, bias_ref, weight_ref), small_sems)
    for t in range(CHUNKS):
        pltpu.make_async_copy(pair_ref.at[:, pl.ds(t * CHUNK, CHUNK), :], held.at[t], sems.at[t]).start()
    for copy in small:
        copy.wait()
    for m in range(4):
        turned = (0.5 * weight_ref[:, m * C : (m + 1) * C].astype(F32)).T.astype(BF16)
        for b in range(C // 16):
            at = 2 * C * (m // 2) + 32 * b + 16 * (m % 2)
            weight_t[at : at + 16, :] = turned[16 * b : 16 * b + 16]
    gain, bias = gain_ref[...], bias_ref[...]

    def product(x, side):
        both = lax.dot_general(
            weight_t[side * 2 * C : (side + 1) * 2 * C, :], x, (((1,), (1,)), ((), ())), preferred_element_type=F32
        )
        both = both.reshape(C // 16, 2, 16, x.shape[0])
        return (both[:, 0] * jnp.tanh(both[:, 1]) + both[:, 0]).reshape(C, x.shape[0])

    @pl.loop(0, CHUNKS)
    def _(t):
        pltpu.make_async_copy(pair_ref.at[:, pl.ds(t * CHUNK, CHUNK), :], held.at[t], sems.at[t]).wait()
        group = 8
        for n in range(ROWS // group):
            block = held[t, n * group : (n + 1) * group].reshape(group * CHUNK, C).astype(F32)
            block = layer_norm(block, gain, bias, -1)
            for u in range(group):
                at = (n * group + u) * STEP
                normed[at : at + CHUNK, :] = block[u * CHUNK : (u + 1) * CHUNK]
        for n in range(CHUNK // 2):
            x = jnp.concatenate(
                [normed[pl.ds(2 * n + e, LANES, stride=STEP), :] for e in range(2)], axis=0
            ).astype(BF16)
            for side in range(2):
                value = product(x, side)
                for e in range(2):
                    dense[side, pl.ds(2 * n + e, C, stride=STEP), :] = value[:, e * 128 : (e + 1) * 128]
        for n in range(CHUNK // 8):
            x = jnp.concatenate(
                [normed[pl.ds(LANES * STEP + 8 * n + e, REST, stride=STEP), :] for e in range(8)], axis=0
            ).astype(BF16)
            for side in range(2):
                value = product(x, side)
                for e in range(2):
                    at = side * TAIL + 4 * t + 2 * n + e
                    tail[pl.ds(at, C, stride=TAIL_STEP), :] = value[:, e * 128 : (e + 1) * 128]
        for side in range(2):
            to = pl.multiple_of(side * COLS + t * CHUNK, CHUNK)
            for h in range(C):
                out_ref[OUT_OF_CHANNEL[h], pl.ds(to, CHUNK), :] = dense[side, h * STEP : h * STEP + CHUNK, :].astype(BF16)

    for h in range(C):
        out_ref[OUT_OF_CHANNEL[h], 2 * COLS :, :] = tail[h * TAIL_STEP : h * TAIL_STEP + 2 * TAIL, :].astype(BF16)


def edges(pair, gain, bias, weight):
    vmem, hbm = pl.BlockSpec(memory_space=pltpu.VMEM), pl.BlockSpec(memory_space=pltpu.HBM)
    return pl.pallas_call(
        edges_kernel,
        in_specs=[hbm] * 4,
        out_specs=vmem,
        out_shape=jax.ShapeDtypeStruct((C, BOTH, LANES), BF16),
        scratch_shapes=[
            pltpu.VMEM((1, C), F32),
            pltpu.VMEM((1, C), F32),
            pltpu.VMEM((C, 4 * C), BF16),
            pltpu.VMEM((4 * C, C), BF16),
            pltpu.VMEM((CHUNKS, ROWS, CHUNK, C), BF16),
            pltpu.VMEM((ROWS * STEP, C), F32),
            pltpu.VMEM((2, C * STEP, LANES), F32),
            pltpu.VMEM((C * TAIL_STEP, LANES), F32),
            pltpu.SemaphoreType.DMA((CHUNKS,)),
            pltpu.SemaphoreType.DMA((3,)),
        ],
        compiler_params=pltpu.CompilerParams(vmem_limit_bytes=VMEM_BYTES),
        cost_estimate=pl.CostEstimate(flops=2 * ROWS * COLS * C * 4 * C, bytes_accessed=10 * MIB, transcendentals=0),
        name="edges",
    )(*in_hbm(pair, gain[None, :], bias[None, :], weight))


def gate_kernel(
    pair_ref, gain_hbm, bias_hbm, weight_hbm, out_hbm, gain_ref, bias_ref, weight_ref, held, out_ref, sems
):
    for copy in fetch((pair_ref, gain_hbm, bias_hbm, weight_hbm), (held, gain_ref, bias_ref, weight_ref), sems):
        copy.wait()
    gain, bias, weight = gain_ref[...], bias_ref[...], weight_ref[...]
    group = 4

    @pl.loop(0, ROWS // group, unroll=2)
    def _(n):
        block = held[pl.ds(n * group, group)].reshape(group * COLS, C).astype(F32)
        normed = layer_norm(block, gain, bias, -1).astype(BF16)
        value = jax.nn.sigmoid(jnp.dot(normed, weight, preferred_element_type=F32))
        out_ref[pl.ds(n * group, group)] = value.astype(BF16).reshape(group, COLS, C)

    store = pltpu.make_async_copy(out_ref, out_hbm, sems.at[4])
    store.start()
    store.wait()


def gates(pair, gain, bias, weight):
    hbm = pl.BlockSpec(memory_space=pltpu.HBM)
    return pl.pallas_call(
        gate_kernel,
        in_specs=[hbm] * 4,
        out_specs=hbm,
        out_shape=pltpu.HBM((ROWS, COLS, C), BF16),
        scratch_shapes=[
            pltpu.VMEM((1, C), F32),
            pltpu.VMEM((1, C), F32),
            pltpu.VMEM((C, C), BF16),
            pltpu.VMEM((ROWS, COLS, C), BF16),
            pltpu.VMEM((ROWS, COLS, C), BF16),
            pltpu.SemaphoreType.DMA((5,)),
        ],
        compiler_params=pltpu.CompilerParams(vmem_limit_bytes=VMEM_BYTES),
        cost_estimate=pl.CostEstimate(flops=2 * ROWS * COLS * C * C, bytes_accessed=30 * MIB, transcendentals=0),
        name="gates",
    )(*in_hbm(pair, gain[None, :], bias[None, :], weight))


def regroup(pieces, lane):
    out = []
    for b in range(PACK):
        total = None
        for a in range(PACK):
            shift = ((a - b) * REST) % LANES
            moved = pltpu.roll(pieces[a], shift, 1) if shift else pieces[a]
            total = moved if total is None else jnp.where(lane // REST == a, moved, total)
        out.append(total)
    return out


def triangle_kernel(edges_ref, out_hbm, left_rest, right_t, rest_left, rest_right, tri_rest, out_ref, sem):
    lane = lax.broadcasted_iota(jnp.int32, (2 * TAIL, LANES), 1)
    for c in range(N_CHAN):
        for q in range(N_ROW // PACK):
            blocks = [FROM_BLOCK[(q * PACK + a) * N_CHAN + c] for a in range(PACK)]
            pieces = [edges_ref[block, 2 * COLS :, :].astype(F32) for block in blocks]
            for b, value in enumerate(regroup(pieces, lane)):
                rest_left[q, pl.ds(c * COLS + b, TAIL, stride=PACK), :] = value[:TAIL]
                rest_right[q, pl.ds(c * COLS + b, TAIL, stride=PACK), :] = value[TAIL:]

    def side(r, first):
        blocks = FROM_BLOCK[r * N_CHAN : (r + 1) * N_CHAN]
        return jnp.concatenate([edges_ref[block, first : first + COLS, :] for block in blocks], axis=0)

    for q in range(N_ROW // PACK):
        left_rest[:, q * LANES : (q + 1) * LANES] = rest_left[q].astype(BF16)
        turned = rest_right[q].astype(BF16).T
        for a in range(PACK):
            at = (q * PACK + a) * ROWS + LANES
            right_t[at : at + REST, :] = turned[a * REST : (a + 1) * REST]
    for r in range(N_ROW):
        right_t[r * ROWS : r * ROWS + LANES, :] = side(r, COLS).T

    part = jnp.dot(right_t[...], left_rest[...], preferred_element_type=F32)
    for q in range(N_ROW // PACK):
        tri_rest[q] = part[:, q * LANES : (q + 1) * LANES]
    lane = lax.broadcasted_iota(jnp.int32, (TAIL, LANES), 1)
    for n in range(N_ROW // 2):
        q = n // 2
        if n % 2 == 0:
            for c in range(N_CHAN):
                pieces = [tri_rest[q, pl.ds(c * COLS + b, TAIL, stride=PACK), :] for b in range(PACK)]
                for a, value in enumerate(regroup(pieces, lane)):
                    value = jnp.concatenate([value, jnp.zeros((BACK - COLS - TAIL, LANES), F32)], axis=0)
                    out_ref[BACK_TO_BLOCK[(q * PACK + a) * N_CHAN + c], COLS:, :] = value.astype(BF16)
        pair = jnp.concatenate([side(2 * n, 0), side(2 * n + 1, 0)], axis=1)
        part = jnp.dot(right_t[...], pair, preferred_element_type=F32).astype(BF16)
        for e in range(2):
            r = 2 * n + e
            for c in range(N_CHAN):
                to = BACK_TO_BLOCK[r * N_CHAN + c]
                out_ref[to, :COLS, :] = part[c * COLS : (c + 1) * COLS, e * LANES : (e + 1) * LANES]
                pltpu.make_async_copy(out_ref.at[to], out_hbm.at[to], sem).start()
    pltpu.make_async_copy(out_ref, out_hbm, sem).wait()


def triangle(edges_all):
    vmem = pl.BlockSpec(memory_space=pltpu.VMEM)
    return pl.pallas_call(
        triangle_kernel,
        in_specs=[vmem],
        out_specs=pl.BlockSpec(memory_space=pltpu.HBM),
        out_shape=pltpu.HBM((N_ROW * N_CHAN, BACK, LANES), BF16),
        scratch_shapes=[
            pltpu.VMEM((SIDE, 2 * LANES), BF16),
            pltpu.VMEM((SIDE, SIDE), BF16),
            pltpu.VMEM((N_ROW // PACK, SIDE, LANES), F32),
            pltpu.VMEM((N_ROW // PACK, SIDE, LANES), F32),
            pltpu.VMEM((N_ROW // PACK, SIDE, LANES), F32),
            pltpu.VMEM((N_ROW * N_CHAN, BACK, LANES), BF16),
            pltpu.SemaphoreType.DMA,
        ],
        compiler_params=pltpu.CompilerParams(vmem_limit_bytes=VMEM_BYTES),
        cost_estimate=pl.CostEstimate(flops=2 * SIDE**3, bytes_accessed=10 * MIB, transcendentals=0),
        name="triangle",
    )(edges_all)


def finish_kernel(
    held, gate_hbm, gain_hbm, bias_hbm, weight_hbm, out_ref, gate_ref, gain_ref, bias_ref, weight_ref, wide, dense, tail, done,
    sems, small_sems
):
    def store(t):
        rows = pl.ds(pl.multiple_of(t * CHUNK, CHUNK), CHUNK)
        return pltpu.make_async_copy(
            done.at[pl.ds(0, LANES), rows, :], out_ref.at[pl.ds(0, LANES), rows, :], sems.at[CHUNKS + 1]
        )

    def load(t):
        rows = pl.ds(pl.multiple_of(t * CHUNK, CHUNK), CHUNK)
        return pltpu.make_async_copy(
            gate_hbm.at[pl.ds(0, LANES), rows, :], gate_ref.at[pl.ds(0, LANES), rows, :], sems.at[t]
        )

    rest = pl.ds(LANES, REST)
    small = fetch((gain_hbm, bias_hbm, weight_hbm), (gain_ref, bias_ref, weight_ref), small_sems)
    for t in range(CHUNKS):
        load(t).start()
    gate_tail = pltpu.make_async_copy(gate_hbm.at[rest], gate_ref.at[rest], sems.at[CHUNKS])
    gate_tail.start()
    for h in range(C):
        wide[h * STEP : h * STEP + TAIL, :] = held[h, COLS:, :].astype(F32)[:TAIL]
    for copy in small:
        copy.wait()
    gain = jnp.broadcast_to(gain_ref[...], (LANES, C)).T
    bias = jnp.broadcast_to(bias_ref[...], (LANES, C)).T
    weight = weight_ref[...]

    def project(g):
        normed = layer_norm(wide[pl.ds(g, C, stride=STEP), :], gain, bias, 0).astype(BF16)
        return lax.dot_general(normed, weight, (((0,), (0,)), ((), ())), preferred_element_type=F32)

    for m in range(TAIL):
        value = project(m)
        for e in range(PACK):
            tail[pl.ds(PACK * m + e, REST, stride=COLS_STEP), :] = value[e * REST : (e + 1) * REST]

    @pl.loop(0, CHUNKS)
    def _(t):
        load(t).wait()
        to = pl.multiple_of(t * CHUNK, CHUNK)
        for h in range(C):
            wide[h * STEP : h * STEP + CHUNK, :] = held[h, pl.ds(to, CHUNK), :].astype(F32)
        for g in range(CHUNK):
            dense[pl.ds(g, LANES, stride=STEP), :] = project(g)
        for i in range(LANES):
            gate = gate_ref[i, pl.ds(to, CHUNK), :].astype(F32)
            done[i, pl.ds(to, CHUNK), :] = (gate * dense[i * STEP : i * STEP + CHUNK, :]).astype(BF16)
        store(t).start()

    gate_tail.wait()
    for i in range(REST):
        gate = gate_ref[LANES + i].astype(F32)
        done[LANES + i] = (gate * tail[i * COLS_STEP : i * COLS_STEP + COLS, :]).astype(BF16)
    last = pltpu.make_async_copy(done.at[rest], out_ref.at[rest], sems.at[CHUNKS + 2])
    last.start()
    last.wait()
    for t in range(CHUNKS):
        store(t).wait()


def finish(tri, gate, gain, bias, weight):
    vmem, hbm = pl.BlockSpec(memory_space=pltpu.VMEM), pl.BlockSpec(memory_space=pltpu.HBM)
    return pl.pallas_call(
        finish_kernel,
        in_specs=[vmem, hbm, hbm, hbm, hbm],
        out_specs=hbm,
        out_shape=jax.ShapeDtypeStruct((ROWS, COLS, C), BF16),
        scratch_shapes=[
            pltpu.VMEM((ROWS, COLS, C), BF16),
            pltpu.VMEM((1, C), F32),
            pltpu.VMEM((1, C), F32),
            pltpu.VMEM((C, C), BF16),
            pltpu.VMEM((C * STEP, LANES), F32),
            pltpu.VMEM((LANES * STEP, C), F32),
            pltpu.VMEM((REST * COLS_STEP, C), F32),
            pltpu.VMEM((ROWS, COLS, C), BF16),
            pltpu.SemaphoreType.DMA((CHUNKS + 3,)),
            pltpu.SemaphoreType.DMA((3,)),
        ],
        compiler_params=pltpu.CompilerParams(vmem_limit_bytes=VMEM_BYTES),
        cost_estimate=pl.CostEstimate(flops=2 * ROWS * COLS * C * C, bytes_accessed=10 * MIB, transcendentals=0),
        name="finish",
    )(tri, *in_hbm(gate, gain[None, :], bias[None, :], weight))


def shards(pair, in_gain, in_bias, edge_weight, gate_weight, out_gain, out_bias, out_weight):
    both = edges(pair, in_gain, in_bias, edge_weight)
    both_all = lax.all_to_all(both, OUT_ORDER, split_axis=0, concat_axis=0, tiled=True)
    gate = gates(pair, in_gain, in_bias, gate_weight)
    tri = lax.all_to_all(triangle(both_all), BACK_ORDER, split_axis=0, concat_axis=0, tiled=True)
    return finish(tri, gate, out_gain, out_bias, out_weight)


def solution(mesh):
    apart = Mesh(mesh.devices.reshape(tuple(SIZES.values())), tuple(SIZES))
    return jax.shard_map(
        shards,
        mesh=apart,
        in_specs=(P(ROW, CHAN, None), P(), P(), P(), P(), P(), P(), P()),
        out_specs=P(ROW, CHAN, None),
        check_vma=False,
    )
```

```python
import jax
import jax.numpy as jnp
from jax import lax
from jax.experimental import pallas as pl
from jax.experimental.pallas import tpu as pltpu
from jax.sharding import Mesh, PartitionSpec as P

ROWS, COLS, C = 160, 80, 128
LANES = 128
REST = ROWS - LANES
PACK = LANES // REST
TAIL = COLS // PACK
CHUNK = 16
CHUNKS = COLS // CHUNK
STEP = CHUNK + 4
TAIL_STEP = 2 * TAIL + 4
COLS_STEP = COLS + 4
BOTH = 2 * (COLS + TAIL)
BACK = 104
N_ROW, N_CHAN = 8, 16
HALF = N_CHAN // 2
SIZES = {"y": 4, "z_lo": 2, "core": 2, "z_hi": 2, "x": 4}
ROW, CHAN = ("z_hi", "x"), ("y", "z_lo", "core")
OUT_ORDER = ROW + CHAN
BACK_ORDER = ("y", "x", "core", "z_lo", "z_hi")
SIDE = 1280
F32, BF16 = jnp.float32, jnp.bfloat16
MIB = 1 << 20
VMEM_BYTES = 36 * MIB


def places(order, inside):
    found = []
    for n in range(N_ROW * N_CHAN):
        at = {}
        for axis in reversed(inside):
            n, at[axis] = divmod(n, SIZES[axis])
        number = 0
        for axis in order:
            number = number * SIZES[axis] + at[axis]
        found.append(number)
    return found


OUT_OF_CHANNEL = places(OUT_ORDER, BACK_ORDER)
FROM_BLOCK = places(OUT_ORDER, ROW + CHAN)
BACK_TO_BLOCK = places(BACK_ORDER, ROW + CHAN)


def layer_norm(values, gain, bias, axis):
    mean = jnp.mean(values, axis=axis, keepdims=True)
    centred = values - mean
    var = jnp.mean(centred * centred, axis=axis, keepdims=True)
    return centred * lax.rsqrt(var + 1e-05) * gain + bias


def in_hbm(*arrays):
    return [pltpu.with_memory_space_constraint(array, pltpu.HBM) for array in arrays]


def fetch(sources, targets, sems):
    copies = [pltpu.make_async_copy(src, dst, sems.at[n]) for n, (src, dst) in enumerate(zip(sources, targets))]
    for copy in copies:
        copy.start()
    return copies


def edges_kernel(
    pair_ref, gain_hbm, bias_hbm, weight_hbm, out_ref, gain_ref, bias_ref, weight_ref, weight_t, held, normed, dense,
    tail, sems, small_sems
):
    small = fetch((gain_hbm, bias_hbm, weight_hbm), (gain_ref, bias_ref, weight_ref), small_sems)
    for t in range(CHUNKS):
        pltpu.make_async_copy(pair_ref.at[:, pl.ds(t * CHUNK, CHUNK), :], held.at[t], sems.at[t]).start()
    for copy in small:
        copy.wait()
    for m in range(4):
        columns = (0.5 * weight_ref[:, m * C : (m + 1) * C].astype(F32)).T.astype(BF16)
        for b in range(C // 16):
            at = 2 * C * (m // 2) + 32 * b + 16 * (m % 2)
            weight_t[at : at + 16, :] = columns[16 * b : 16 * b + 16]
    gain, bias = gain_ref[...], bias_ref[...]
    average = jnp.full((C, C), 1 / C, BF16)
    turn = lax.axis_index("x")

    def product(x, side):
        both = lax.dot_general(
            weight_t[side * 2 * C : (side + 1) * 2 * C, :], x, (((1,), (1,)), ((), ())), preferred_element_type=F32
        )
        both = both.reshape(C // 16, 2, 16, x.shape[0])
        return (both[:, 0] * jnp.tanh(both[:, 1]) + both[:, 0]).reshape(C, x.shape[0])

    @pl.loop(0, CHUNKS)
    def _(t):
        pltpu.make_async_copy(pair_ref.at[:, pl.ds(t * CHUNK, CHUNK), :], held.at[t], sems.at[t]).wait()
        group = 8
        for n in range(ROWS // group):
            block = held[t, n * group : (n + 1) * group].reshape(group * CHUNK, C)
            centred = block.astype(F32) - jnp.dot(block, average, preferred_element_type=F32)
            var = jnp.mean(centred * centred, axis=-1, keepdims=True)
            block = centred * lax.rsqrt(var + 1e-05) * gain + bias
            for u in range(group):
                at = (n * group + u) * STEP
                normed[at : at + CHUNK, :] = block[u * CHUNK : (u + 1) * CHUNK]
        for n in range(CHUNK // 2):
            x = jnp.concatenate(
                [normed[pl.ds(2 * n + e, LANES, stride=STEP), :] for e in range(2)], axis=0
            ).astype(BF16)
            for side in range(2):
                value = product(x, side)
                for e in range(2):
                    dense[side, pl.ds(2 * n + e, C, stride=STEP), :] = value[:, e * 128 : (e + 1) * 128]
        for n in range(CHUNK // 8):
            x = jnp.concatenate(
                [
                    normed[pl.ds(LANES * STEP + 8 * n + u + lax.rem(g + PACK - turn, PACK), REST, stride=STEP), :]
                    for u in (0, PACK)
                    for g in range(PACK)
                ],
                axis=0,
            ).astype(BF16)
            for side in range(2):
                value = product(x, side)
                for e in range(2):
                    at = side * TAIL + 4 * t + 2 * n + e
                    tail[pl.ds(at, C, stride=TAIL_STEP), :] = value[:, e * 128 : (e + 1) * 128]
        for side in range(2):
            to = pl.multiple_of(side * COLS + t * CHUNK, CHUNK)
            for h in range(C):
                out_ref[OUT_OF_CHANNEL[h], pl.ds(to, CHUNK), :] = dense[side, h * STEP : h * STEP + CHUNK, :].astype(BF16)

    for h in range(C):
        out_ref[OUT_OF_CHANNEL[h], 2 * COLS :, :] = tail[h * TAIL_STEP : h * TAIL_STEP + 2 * TAIL, :].astype(BF16)


def edges(pair, gain, bias, weight):
    vmem, hbm = pl.BlockSpec(memory_space=pltpu.VMEM), pl.BlockSpec(memory_space=pltpu.HBM)
    return pl.pallas_call(
        edges_kernel,
        in_specs=[hbm] * 4,
        out_specs=vmem,
        out_shape=jax.ShapeDtypeStruct((C, BOTH, LANES), BF16),
        scratch_shapes=[
            pltpu.VMEM((1, C), F32),
            pltpu.VMEM((1, C), F32),
            pltpu.VMEM((C, 4 * C), BF16),
            pltpu.VMEM((4 * C, C), BF16),
            pltpu.VMEM((CHUNKS, ROWS, CHUNK, C), BF16),
            pltpu.VMEM((ROWS * STEP, C), F32),
            pltpu.VMEM((2, C * STEP, LANES), F32),
            pltpu.VMEM((C * TAIL_STEP, LANES), F32),
            pltpu.SemaphoreType.DMA((CHUNKS,)),
            pltpu.SemaphoreType.DMA((3,)),
        ],
        compiler_params=pltpu.CompilerParams(vmem_limit_bytes=VMEM_BYTES),
        cost_estimate=pl.CostEstimate(flops=2 * ROWS * COLS * C * 4 * C, bytes_accessed=10 * MIB, transcendentals=0),
        name="edges",
    )(*in_hbm(pair, gain[None, :], bias[None, :], weight))


def gate_kernel(
    pair_ref, gain_hbm, bias_hbm, weight_hbm, out_hbm, gain_ref, bias_ref, weight_ref, held, out_ref, sems
):
    for copy in fetch((pair_ref, gain_hbm, bias_hbm, weight_hbm), (held, gain_ref, bias_ref, weight_ref), sems):
        copy.wait()
    gain, bias, weight = gain_ref[...], bias_ref[...], weight_ref[...]
    group = 4

    @pl.loop(0, ROWS // group, unroll=2)
    def _(n):
        block = held[pl.ds(n * group, group)].reshape(group * COLS, C).astype(F32)
        normed = layer_norm(block, gain, bias, -1).astype(BF16)
        value = jax.nn.sigmoid(jnp.dot(normed, weight, preferred_element_type=F32))
        out_ref[pl.ds(n * group, group)] = value.astype(BF16).reshape(group, COLS, C)

    store = pltpu.make_async_copy(out_ref, out_hbm, sems.at[4])
    store.start()
    store.wait()


def gates(pair, gain, bias, weight):
    hbm = pl.BlockSpec(memory_space=pltpu.HBM)
    return pl.pallas_call(
        gate_kernel,
        in_specs=[hbm] * 4,
        out_specs=hbm,
        out_shape=pltpu.HBM((ROWS, COLS, C), BF16),
        scratch_shapes=[
            pltpu.VMEM((1, C), F32),
            pltpu.VMEM((1, C), F32),
            pltpu.VMEM((C, C), BF16),
            pltpu.VMEM((ROWS, COLS, C), BF16),
            pltpu.VMEM((ROWS, COLS, C), BF16),
            pltpu.SemaphoreType.DMA((5,)),
        ],
        compiler_params=pltpu.CompilerParams(vmem_limit_bytes=VMEM_BYTES),
        cost_estimate=pl.CostEstimate(flops=2 * ROWS * COLS * C * C, bytes_accessed=30 * MIB, transcendentals=0),
        name="gates",
    )(*in_hbm(pair, gain[None, :], bias[None, :], weight))


def choose(lane, pieces):
    out = pieces[0]
    for g in range(1, PACK):
        out = jnp.where(lane // REST == g, pieces[g], out)
    return out


def turned(value, groups):
    return pltpu.roll(value, groups * REST, 1) if groups else value


def triangle_kernel(edges_ref, out_hbm, left_rest, right_t, rest_left, rest_right, tri_rest, out_ref, sem):
    lane = lax.broadcasted_iota(jnp.int32, (2 * TAIL, LANES), 1)
    for c in range(N_CHAN):
        for q in range(N_ROW // PACK):
            blocks = [FROM_BLOCK[(q * PACK + a) * N_CHAN + c] for a in range(PACK)]
            pieces = [edges_ref[block, 2 * COLS :, :].astype(F32) for block in blocks]
            for b in range(PACK):
                value = turned(choose(lane, [pieces[(g - b) % PACK] for g in range(PACK)]), -b % PACK)
                rest_left[q, pl.ds(c * COLS + b, TAIL, stride=PACK), :] = value[:TAIL]
                rest_right[q, pl.ds(c * COLS + b, TAIL, stride=PACK), :] = value[TAIL:]

    def side(r, first):
        blocks = FROM_BLOCK[r * N_CHAN : (r + 1) * N_CHAN]
        return jnp.concatenate([edges_ref[block, first : first + COLS, :] for block in blocks], axis=0)

    for q in range(N_ROW // PACK):
        left_rest[:, q * LANES : (q + 1) * LANES] = rest_left[q].astype(BF16)
        columns = rest_right[q].astype(BF16).T
        for a in range(PACK):
            at = (q * PACK + a) * ROWS + LANES
            right_t[at : at + REST, :] = columns[a * REST : (a + 1) * REST]
    for r in range(N_ROW):
        right_t[r * ROWS : r * ROWS + LANES, :] = side(r, COLS).T

    for first in range(0, N_CHAN, HALF):
        rows = pl.ds(first * COLS, HALF * COLS)
        part = jnp.dot(right_t[rows, :], left_rest[...], preferred_element_type=F32)
        for q in range(N_ROW // PACK):
            tri_rest[q, rows, :] = part[:, q * LANES : (q + 1) * LANES]
    lane = lax.broadcasted_iota(jnp.int32, (TAIL, LANES), 1)
    for n in range(N_ROW // 2):
        q = n // 2
        if n % 2 == 0:
            for c in range(N_CHAN):
                pieces = [tri_rest[q, pl.ds(c * COLS + b, TAIL, stride=PACK), :] for b in range(PACK)]
                pieces = [turned(piece, b) for b, piece in enumerate(pieces)]
                for a in range(PACK):
                    value = choose(lane, [pieces[(g - a) % PACK] for g in range(PACK)])
                    value = jnp.concatenate([value, jnp.zeros((BACK - COLS - TAIL, LANES), F32)], axis=0)
                    out_ref[BACK_TO_BLOCK[(q * PACK + a) * N_CHAN + c], COLS:, :] = value.astype(BF16)
        pair = jnp.concatenate([side(2 * n, 0), side(2 * n + 1, 0)], axis=1)
        for first in range(0, N_CHAN, HALF):
            rows = right_t[first * COLS : (first + HALF) * COLS]
            part = jnp.dot(rows, pair, preferred_element_type=F32).astype(BF16)
            for e in range(2):
                for c in range(HALF):
                    to = BACK_TO_BLOCK[(2 * n + e) * N_CHAN + first + c]
                    out_ref[to, :COLS, :] = part[c * COLS : (c + 1) * COLS, e * LANES : (e + 1) * LANES]
                    pltpu.make_async_copy(out_ref.at[to], out_hbm.at[to], sem).start()
    pltpu.make_async_copy(out_ref, out_hbm, sem).wait()


def triangle(edges_all):
    vmem = pl.BlockSpec(memory_space=pltpu.VMEM)
    return pl.pallas_call(
        triangle_kernel,
        in_specs=[vmem],
        out_specs=pl.BlockSpec(memory_space=pltpu.HBM),
        out_shape=pltpu.HBM((N_ROW * N_CHAN, BACK, LANES), BF16),
        scratch_shapes=[
            pltpu.VMEM((SIDE, 2 * LANES), BF16),
            pltpu.VMEM((SIDE, SIDE), BF16),
            pltpu.VMEM((N_ROW // PACK, SIDE, LANES), F32),
            pltpu.VMEM((N_ROW // PACK, SIDE, LANES), F32),
            pltpu.VMEM((N_ROW // PACK, SIDE, LANES), F32),
            pltpu.VMEM((N_ROW * N_CHAN, BACK, LANES), BF16),
            pltpu.SemaphoreType.DMA,
        ],
        compiler_params=pltpu.CompilerParams(vmem_limit_bytes=VMEM_BYTES),
        cost_estimate=pl.CostEstimate(flops=2 * SIDE**3, bytes_accessed=10 * MIB, transcendentals=0),
        name="triangle",
    )(edges_all)


def finish_kernel(
    held, gate_hbm, gain_hbm, bias_hbm, weight_hbm, out_ref, gate_ref, gain_ref, bias_ref, weight_ref, wide, dense, tail, done,
    sems, small_sems
):
    def store(t):
        rows = pl.ds(pl.multiple_of(t * CHUNK, CHUNK), CHUNK)
        return pltpu.make_async_copy(
            done.at[pl.ds(0, LANES), rows, :], out_ref.at[pl.ds(0, LANES), rows, :], sems.at[CHUNKS + 1]
        )

    def load(t):
        rows = pl.ds(pl.multiple_of(t * CHUNK, CHUNK), CHUNK)
        return pltpu.make_async_copy(
            gate_hbm.at[pl.ds(0, LANES), rows, :], gate_ref.at[pl.ds(0, LANES), rows, :], sems.at[t]
        )

    rest = pl.ds(LANES, REST)
    small = fetch((gain_hbm, bias_hbm, weight_hbm), (gain_ref, bias_ref, weight_ref), small_sems)
    gate_tail = pltpu.make_async_copy(gate_hbm.at[rest], gate_ref.at[rest], sems.at[CHUNKS])
    gate_tail.start()
    for t in range(CHUNKS):
        load(t).start()
    turn = lax.axis_index("x")
    for h in range(C):
        wide[h * STEP : h * STEP + TAIL, :] = held[h, COLS:, :].astype(F32)[:TAIL]
    for copy in small:
        copy.wait()
    gain = jnp.broadcast_to(gain_ref[...], (LANES, C)).T
    bias = jnp.broadcast_to(bias_ref[...], (LANES, C)).T
    weight = weight_ref[...]

    def project(g):
        normed = layer_norm(wide[pl.ds(g, C, stride=STEP), :], gain, bias, 0).astype(BF16)
        return lax.dot_general(normed, weight, (((0,), (0,)), ((), ())), preferred_element_type=F32)

    for m in range(TAIL):
        value = project(m)
        for g in range(PACK):
            at = PACK * m + lax.rem(g + PACK - turn, PACK)
            tail[pl.ds(at, REST, stride=COLS_STEP), :] = value[g * REST : (g + 1) * REST]
    gate_tail.wait()
    for i in range(REST):
        gate = gate_ref[LANES + i].astype(F32)
        done[LANES + i] = (gate * tail[i * COLS_STEP : i * COLS_STEP + COLS, :]).astype(BF16)
    last = pltpu.make_async_copy(done.at[rest], out_ref.at[rest], sems.at[CHUNKS + 2])
    last.start()

    @pl.loop(0, CHUNKS)
    def _(t):
        load(t).wait()
        to = pl.multiple_of(t * CHUNK, CHUNK)
        for h in range(C):
            wide[h * STEP : h * STEP + CHUNK, :] = held[h, pl.ds(to, CHUNK), :].astype(F32)
        for g in range(CHUNK):
            dense[pl.ds(g, LANES, stride=STEP), :] = project(g)
        for i in range(LANES):
            gate = gate_ref[i, pl.ds(to, CHUNK), :].astype(F32)
            done[i, pl.ds(to, CHUNK), :] = (gate * dense[i * STEP : i * STEP + CHUNK, :]).astype(BF16)
        store(t).start()

    last.wait()
    for t in range(CHUNKS):
        store(t).wait()


def finish(tri, gate, gain, bias, weight):
    vmem, hbm = pl.BlockSpec(memory_space=pltpu.VMEM), pl.BlockSpec(memory_space=pltpu.HBM)
    return pl.pallas_call(
        finish_kernel,
        in_specs=[vmem, hbm, hbm, hbm, hbm],
        out_specs=hbm,
        out_shape=jax.ShapeDtypeStruct((ROWS, COLS, C), BF16),
        scratch_shapes=[
            pltpu.VMEM((ROWS, COLS, C), BF16),
            pltpu.VMEM((1, C), F32),
            pltpu.VMEM((1, C), F32),
            pltpu.VMEM((C, C), BF16),
            pltpu.VMEM((C * STEP, LANES), F32),
            pltpu.VMEM((LANES * STEP, C), F32),
            pltpu.VMEM((REST * COLS_STEP, C), F32),
            pltpu.VMEM((ROWS, COLS, C), BF16),
            pltpu.SemaphoreType.DMA((CHUNKS + 3,)),
            pltpu.SemaphoreType.DMA((3,)),
        ],
        compiler_params=pltpu.CompilerParams(vmem_limit_bytes=VMEM_BYTES),
        cost_estimate=pl.CostEstimate(flops=2 * ROWS * COLS * C * C, bytes_accessed=10 * MIB, transcendentals=0),
        name="finish",
    )(tri, *in_hbm(gate, gain[None, :], bias[None, :], weight))


def shards(pair, in_gain, in_bias, edge_weight, gate_weight, out_gain, out_bias, out_weight):
    both = edges(pair, in_gain, in_bias, edge_weight)
    both_all = lax.all_to_all(both, OUT_ORDER, split_axis=0, concat_axis=0, tiled=True)
    gate = gates(pair, in_gain, in_bias, gate_weight)
    tri = lax.all_to_all(triangle(both_all), BACK_ORDER, split_axis=0, concat_axis=0, tiled=True)
    return finish(tri, gate, out_gain, out_bias, out_weight)


def solution(mesh):
    apart = Mesh(mesh.devices.reshape(tuple(SIZES.values())), tuple(SIZES))
    return jax.shard_map(
        shards,
        mesh=apart,
        in_specs=(P(ROW, CHAN, None), P(), P(), P(), P(), P(), P(), P()),
        out_specs=P(ROW, CHAN, None),
        check_vma=False,
    )
```

```python
import jax
import jax.numpy as jnp
from jax import lax
from jax.experimental import pallas as pl
from jax.experimental.pallas import tpu as pltpu
from jax.sharding import Mesh, PartitionSpec as P

ROWS, COLS, C = 160, 80, 128
LANES = 128
REST = ROWS - LANES
PACK = LANES // REST
TAIL = COLS // PACK
CHUNK = 16
CHUNKS = COLS // CHUNK
STEP = CHUNK + 4
TAIL_STEP = 2 * TAIL + 4
COLS_STEP = COLS + 4
BOTH = 2 * (COLS + TAIL)
BACK = 104
N_ROW, N_CHAN = 8, 16
HALF = N_CHAN // 2
SIZES = {"y": 4, "z_lo": 2, "core": 2, "z_hi": 2, "x": 4}
ROW, CHAN = ("z_hi", "x"), ("y", "z_lo", "core")
OUT_ORDER = ("z_hi", "x", "core", "y", "z_lo")
BACK_ORDER = ("y", "x", "core", "z_lo", "z_hi")
SIDE = 1280
F32, BF16 = jnp.float32, jnp.bfloat16
MIB = 1 << 20
VMEM_BYTES = 36 * MIB


def places(order, inside):
    found = []
    for n in range(N_ROW * N_CHAN):
        at = {}
        for axis in reversed(inside):
            n, at[axis] = divmod(n, SIZES[axis])
        number = 0
        for axis in order:
            number = number * SIZES[axis] + at[axis]
        found.append(number)
    return found


OUT_OF_CHANNEL = places(OUT_ORDER, BACK_ORDER)
FROM_BLOCK = places(OUT_ORDER, ROW + CHAN)
BACK_TO_BLOCK = places(BACK_ORDER, ROW + CHAN)


def layer_norm(values, gain, bias, axis):
    mean = jnp.mean(values, axis=axis, keepdims=True)
    centred = values - mean
    var = jnp.mean(centred * centred, axis=axis, keepdims=True)
    return centred * lax.rsqrt(var + 1e-05) * gain + bias


def in_hbm(*arrays):
    return [pltpu.with_memory_space_constraint(array, pltpu.HBM) for array in arrays]


def fetch(sources, targets, sems):
    copies = [pltpu.make_async_copy(src, dst, sems.at[n]) for n, (src, dst) in enumerate(zip(sources, targets))]
    for copy in copies:
        copy.start()
    return copies


def edges_kernel(
    pair_ref, gain_hbm, bias_hbm, weight_hbm, out_ref, gain_ref, bias_ref, weight_ref, weight_t, held, normed, dense,
    tail, sems, small_sems
):
    small = fetch((gain_hbm, bias_hbm, weight_hbm), (gain_ref, bias_ref, weight_ref), small_sems)
    for t in range(CHUNKS):
        pltpu.make_async_copy(pair_ref.at[:, pl.ds(t * CHUNK, CHUNK), :], held.at[t], sems.at[t]).start()
    for copy in small:
        copy.wait()
    for m in range(4):
        columns = (0.5 * weight_ref[:, m * C : (m + 1) * C].astype(F32)).T.astype(BF16)
        for b in range(C // 16):
            at = 2 * C * (m // 2) + 32 * b + 16 * (m % 2)
            weight_t[at : at + 16, :] = columns[16 * b : 16 * b + 16]
    gain, bias = gain_ref[...], bias_ref[...]
    average = jnp.full((C, C), 1 / C, BF16)
    turn = lax.axis_index("x")

    def product(x, side):
        both = lax.dot_general(
            weight_t[side * 2 * C : (side + 1) * 2 * C, :], x, (((1,), (1,)), ((), ())), preferred_element_type=F32
        )
        both = both.reshape(C // 16, 2, 16, x.shape[0])
        return (both[:, 0] * jnp.tanh(both[:, 1]) + both[:, 0]).reshape(C, x.shape[0])

    @pl.loop(0, CHUNKS)
    def _(t):
        pltpu.make_async_copy(pair_ref.at[:, pl.ds(t * CHUNK, CHUNK), :], held.at[t], sems.at[t]).wait()
        group = 16
        for n in range(ROWS // group):
            block = held[t, n * group : (n + 1) * group].reshape(group * CHUNK, C)
            centred = block.astype(F32) - jnp.dot(block, average, preferred_element_type=F32)
            var = jnp.mean(centred * centred, axis=-1, keepdims=True)
            block = centred * lax.rsqrt(var + 1e-05) * gain + bias
            for u in range(group):
                at = (n * group + u) * STEP
                normed[at : at + CHUNK, :] = block[u * CHUNK : (u + 1) * CHUNK]
        for n in range(CHUNK // 2):
            x = jnp.concatenate(
                [normed[pl.ds(2 * n + e, LANES, stride=STEP), :] for e in range(2)], axis=0
            ).astype(BF16)
            for side in range(2):
                value = product(x, side)
                for e in range(2):
                    dense[side, pl.ds(2 * n + e, C, stride=STEP), :] = value[:, e * 128 : (e + 1) * 128]
        for n in range(CHUNK // 8):
            x = jnp.concatenate(
                [
                    normed[pl.ds(LANES * STEP + 8 * n + u + lax.rem(g + PACK - turn, PACK), REST, stride=STEP), :]
                    for u in (0, PACK)
                    for g in range(PACK)
                ],
                axis=0,
            ).astype(BF16)
            for side in range(2):
                value = product(x, side)
                for e in range(2):
                    at = side * TAIL + 4 * t + 2 * n + e
                    tail[pl.ds(at, C, stride=TAIL_STEP), :] = value[:, e * 128 : (e + 1) * 128]
        for h in range(C):
            for side in range(2):
                to = pl.multiple_of(side * COLS + t * CHUNK, CHUNK)
                out_ref[OUT_OF_CHANNEL[h], pl.ds(to, CHUNK), :] = dense[side, h * STEP : h * STEP + CHUNK, :].astype(BF16)

    for h in range(C):
        out_ref[OUT_OF_CHANNEL[h], 2 * COLS :, :] = tail[h * TAIL_STEP : h * TAIL_STEP + 2 * TAIL, :].astype(BF16)


def edges(pair, gain, bias, weight):
    vmem, hbm = pl.BlockSpec(memory_space=pltpu.VMEM), pl.BlockSpec(memory_space=pltpu.HBM)
    return pl.pallas_call(
        edges_kernel,
        in_specs=[hbm] * 4,
        out_specs=vmem,
        out_shape=jax.ShapeDtypeStruct((C, BOTH, LANES), BF16),
        scratch_shapes=[
            pltpu.VMEM((1, C), F32),
            pltpu.VMEM((1, C), F32),
            pltpu.VMEM((C, 4 * C), BF16),
            pltpu.VMEM((4 * C, C), BF16),
            pltpu.VMEM((CHUNKS, ROWS, CHUNK, C), BF16),
            pltpu.VMEM((ROWS * STEP, C), F32),
            pltpu.VMEM((2, C * STEP, LANES), F32),
            pltpu.VMEM((C * TAIL_STEP, LANES), F32),
            pltpu.SemaphoreType.DMA((CHUNKS,)),
            pltpu.SemaphoreType.DMA((3,)),
        ],
        compiler_params=pltpu.CompilerParams(vmem_limit_bytes=VMEM_BYTES),
        cost_estimate=pl.CostEstimate(flops=2 * ROWS * COLS * C * 4 * C, bytes_accessed=10 * MIB, transcendentals=0),
        name="edges",
    )(*in_hbm(pair, gain[None, :], bias[None, :], weight))


def gate_kernel(
    pair_ref, gain_hbm, bias_hbm, weight_hbm, out_hbm, gain_ref, bias_ref, weight_ref, held, out_ref, sems
):
    for copy in fetch((pair_ref, gain_hbm, bias_hbm, weight_hbm), (held, gain_ref, bias_ref, weight_ref), sems):
        copy.wait()
    gain, bias, weight = gain_ref[...], bias_ref[...], weight_ref[...]
    group = 4

    @pl.loop(0, ROWS // group, unroll=2)
    def _(n):
        block = held[pl.ds(n * group, group)].reshape(group * COLS, C).astype(F32)
        normed = layer_norm(block, gain, bias, -1).astype(BF16)
        value = jax.nn.sigmoid(jnp.dot(normed, weight, preferred_element_type=F32))
        out_ref[pl.ds(n * group, group)] = value.astype(BF16).reshape(group, COLS, C)

    store = pltpu.make_async_copy(out_ref, out_hbm, sems.at[4])
    store.start()
    store.wait()


def gates(pair, gain, bias, weight):
    hbm = pl.BlockSpec(memory_space=pltpu.HBM)
    return pl.pallas_call(
        gate_kernel,
        in_specs=[hbm] * 4,
        out_specs=hbm,
        out_shape=pltpu.HBM((ROWS, COLS, C), BF16),
        scratch_shapes=[
            pltpu.VMEM((1, C), F32),
            pltpu.VMEM((1, C), F32),
            pltpu.VMEM((C, C), BF16),
            pltpu.VMEM((ROWS, COLS, C), BF16),
            pltpu.VMEM((ROWS, COLS, C), BF16),
            pltpu.SemaphoreType.DMA((5,)),
        ],
        compiler_params=pltpu.CompilerParams(vmem_limit_bytes=VMEM_BYTES),
        cost_estimate=pl.CostEstimate(flops=2 * ROWS * COLS * C * C, bytes_accessed=30 * MIB, transcendentals=0),
        name="gates",
    )(*in_hbm(pair, gain[None, :], bias[None, :], weight))


def choose(lane, pieces):
    out = pieces[0]
    for g in range(1, PACK):
        out = jnp.where(lane // REST == g, pieces[g], out)
    return out


def turned(value, groups):
    return pltpu.roll(value, groups * REST, 1) if groups else value


def triangle_kernel(edges_ref, out_hbm, left_rest, right_t, rest_left, rest_right, tri_rest, out_ref, sem):
    lane = lax.broadcasted_iota(jnp.int32, (2 * TAIL, LANES), 1)
    for c in range(N_CHAN):
        for q in range(N_ROW // PACK):
            blocks = [FROM_BLOCK[(q * PACK + a) * N_CHAN + c] for a in range(PACK)]
            pieces = [edges_ref[block, 2 * COLS :, :].astype(F32) for block in blocks]
            for b in range(PACK):
                value = turned(choose(lane, [pieces[(g - b) % PACK] for g in range(PACK)]), -b % PACK)
                rest_left[q, pl.ds(c * COLS + b, TAIL, stride=PACK), :] = value[:TAIL]
                rest_right[q, pl.ds(c * COLS + b, TAIL, stride=PACK), :] = value[TAIL:]

    def side(r, first):
        blocks = FROM_BLOCK[r * N_CHAN : (r + 1) * N_CHAN]
        return jnp.concatenate([edges_ref[block, first : first + COLS, :] for block in blocks], axis=0)

    for q in range(N_ROW // PACK):
        left_rest[:, q * LANES : (q + 1) * LANES] = rest_left[q].astype(BF16)
        columns = rest_right[q].astype(BF16).T
        for a in range(PACK):
            at = (q * PACK + a) * ROWS + LANES
            right_t[at : at + REST, :] = columns[a * REST : (a + 1) * REST]
    for r in range(N_ROW):
        right_t[r * ROWS : r * ROWS + LANES, :] = side(r, COLS).T

    for first in range(0, N_CHAN, HALF):
        rows = pl.ds(first * COLS, HALF * COLS)
        part = jnp.dot(right_t[rows, :], left_rest[...], preferred_element_type=F32)
        for q in range(N_ROW // PACK):
            tri_rest[q, rows, :] = part[:, q * LANES : (q + 1) * LANES]
    lane = lax.broadcasted_iota(jnp.int32, (TAIL, LANES), 1)
    for n in range(N_ROW // 2):
        q = n // 2
        if n % 2 == 0:
            for c in range(N_CHAN):
                pieces = [tri_rest[q, pl.ds(c * COLS + b, TAIL, stride=PACK), :] for b in range(PACK)]
                pieces = [turned(piece, b) for b, piece in enumerate(pieces)]
                for a in range(PACK):
                    value = choose(lane, [pieces[(g - a) % PACK] for g in range(PACK)])
                    value = jnp.concatenate([value, jnp.zeros((BACK - COLS - TAIL, LANES), F32)], axis=0)
                    out_ref[BACK_TO_BLOCK[(q * PACK + a) * N_CHAN + c], COLS:, :] = value.astype(BF16)
        pair = jnp.concatenate([side(2 * n, 0), side(2 * n + 1, 0)], axis=1)
        for first in range(0, N_CHAN, HALF):
            rows = right_t[first * COLS : (first + HALF) * COLS]
            part = jnp.dot(rows, pair, preferred_element_type=F32).astype(BF16)
            for e in range(2):
                for c in range(HALF):
                    to = BACK_TO_BLOCK[(2 * n + e) * N_CHAN + first + c]
                    out_ref[to, :COLS, :] = part[c * COLS : (c + 1) * COLS, e * LANES : (e + 1) * LANES]
                    pltpu.make_async_copy(out_ref.at[to], out_hbm.at[to], sem).start()
    pltpu.make_async_copy(out_ref, out_hbm, sem).wait()


def triangle(edges_all):
    vmem = pl.BlockSpec(memory_space=pltpu.VMEM)
    return pl.pallas_call(
        triangle_kernel,
        in_specs=[vmem],
        out_specs=pl.BlockSpec(memory_space=pltpu.HBM),
        out_shape=pltpu.HBM((N_ROW * N_CHAN, BACK, LANES), BF16),
        scratch_shapes=[
            pltpu.VMEM((SIDE, 2 * LANES), BF16),
            pltpu.VMEM((SIDE, SIDE), BF16),
            pltpu.VMEM((N_ROW // PACK, SIDE, LANES), F32),
            pltpu.VMEM((N_ROW // PACK, SIDE, LANES), F32),
            pltpu.VMEM((N_ROW // PACK, SIDE, LANES), F32),
            pltpu.VMEM((N_ROW * N_CHAN, BACK, LANES), BF16),
            pltpu.SemaphoreType.DMA,
        ],
        compiler_params=pltpu.CompilerParams(vmem_limit_bytes=VMEM_BYTES),
        cost_estimate=pl.CostEstimate(flops=2 * SIDE**3, bytes_accessed=10 * MIB, transcendentals=0),
        name="triangle",
    )(edges_all)


def finish_kernel(
    held, gate_hbm, gain_hbm, bias_hbm, weight_hbm, out_ref, gate_ref, gain_ref, bias_ref, weight_ref, wide, dense, tail, done,
    sems, small_sems
):
    def store(t):
        rows = pl.ds(pl.multiple_of(t * CHUNK, CHUNK), CHUNK)
        return pltpu.make_async_copy(
            done.at[pl.ds(0, LANES), rows, :], out_ref.at[pl.ds(0, LANES), rows, :], sems.at[CHUNKS + 1]
        )

    def load(t):
        rows = pl.ds(pl.multiple_of(t * CHUNK, CHUNK), CHUNK)
        return pltpu.make_async_copy(
            gate_hbm.at[pl.ds(0, LANES), rows, :], gate_ref.at[pl.ds(0, LANES), rows, :], sems.at[t]
        )

    rest = pl.ds(LANES, REST)
    small = fetch((gain_hbm, bias_hbm, weight_hbm), (gain_ref, bias_ref, weight_ref), small_sems)
    gate_tail = pltpu.make_async_copy(gate_hbm.at[rest], gate_ref.at[rest], sems.at[CHUNKS])
    gate_tail.start()
    for t in range(CHUNKS):
        load(t).start()
    turn = lax.axis_index("x")
    for h in range(C):
        wide[h * STEP : h * STEP + TAIL, :] = held[h, COLS:, :].astype(F32)[:TAIL]
    for copy in small:
        copy.wait()
    gain = jnp.broadcast_to(gain_ref[...], (LANES, C)).T
    bias = jnp.broadcast_to(bias_ref[...], (LANES, C)).T
    weight = weight_ref[...]

    def project(g):
        normed = layer_norm(wide[pl.ds(g, C, stride=STEP), :], gain, bias, 0).astype(BF16)
        return lax.dot_general(normed, weight, (((0,), (0,)), ((), ())), preferred_element_type=F32)

    for m in range(TAIL):
        value = project(m)
        for g in range(PACK):
            at = PACK * m + lax.rem(g + PACK - turn, PACK)
            tail[pl.ds(at, REST, stride=COLS_STEP), :] = value[g * REST : (g + 1) * REST]
    gate_tail.wait()
    for i in range(REST):
        gate = gate_ref[LANES + i].astype(F32)
        done[LANES + i] = (gate * tail[i * COLS_STEP : i * COLS_STEP + COLS, :]).astype(BF16)
    last = pltpu.make_async_copy(done.at[rest], out_ref.at[rest], sems.at[CHUNKS + 2])
    last.start()

    @pl.loop(0, CHUNKS)
    def _(t):
        load(t).wait()
        to = pl.multiple_of(t * CHUNK, CHUNK)
        for h in range(C):
            wide[h * STEP : h * STEP + CHUNK, :] = held[h, pl.ds(to, CHUNK), :].astype(F32)
        for g in range(CHUNK):
            dense[pl.ds(g, LANES, stride=STEP), :] = project(g)
        for i in range(LANES):
            gate = gate_ref[i, pl.ds(to, CHUNK), :].astype(F32)
            done[i, pl.ds(to, CHUNK), :] = (gate * dense[i * STEP : i * STEP + CHUNK, :]).astype(BF16)
        store(t).start()

    last.wait()
    for t in range(CHUNKS):
        store(t).wait()


def finish(tri, gate, gain, bias, weight):
    vmem, hbm = pl.BlockSpec(memory_space=pltpu.VMEM), pl.BlockSpec(memory_space=pltpu.HBM)
    return pl.pallas_call(
        finish_kernel,
        in_specs=[vmem, hbm, hbm, hbm, hbm],
        out_specs=hbm,
        out_shape=jax.ShapeDtypeStruct((ROWS, COLS, C), BF16),
        scratch_shapes=[
            pltpu.VMEM((ROWS, COLS, C), BF16),
            pltpu.VMEM((1, C), F32),
            pltpu.VMEM((1, C), F32),
            pltpu.VMEM((C, C), BF16),
            pltpu.VMEM((C * STEP, LANES), F32),
            pltpu.VMEM((LANES * STEP, C), F32),
            pltpu.VMEM((REST * COLS_STEP, C), F32),
            pltpu.VMEM((ROWS, COLS, C), BF16),
            pltpu.SemaphoreType.DMA((CHUNKS + 3,)),
            pltpu.SemaphoreType.DMA((3,)),
        ],
        compiler_params=pltpu.CompilerParams(vmem_limit_bytes=VMEM_BYTES),
        cost_estimate=pl.CostEstimate(flops=2 * ROWS * COLS * C * C, bytes_accessed=10 * MIB, transcendentals=0),
        name="finish",
    )(tri, *in_hbm(gate, gain[None, :], bias[None, :], weight))


def shards(pair, in_gain, in_bias, edge_weight, gate_weight, out_gain, out_bias, out_weight):
    both = edges(pair, in_gain, in_bias, edge_weight)
    both_all = lax.all_to_all(both, OUT_ORDER, split_axis=0, concat_axis=0, tiled=True)
    gate = gates(pair, in_gain, in_bias, gate_weight)
    tri = lax.all_to_all(triangle(both_all), BACK_ORDER, split_axis=0, concat_axis=0, tiled=True)
    return finish(tri, gate, out_gain, out_bias, out_weight)


def solution(mesh):
    apart = Mesh(mesh.devices.reshape(tuple(SIZES.values())), tuple(SIZES))
    return jax.shard_map(
        shards,
        mesh=apart,
        in_specs=(P(ROW, CHAN, None), P(), P(), P(), P(), P(), P(), P()),
        out_specs=P(ROW, CHAN, None),
        check_vma=False,
    )
```

```python
import jax
import jax.numpy as jnp
from jax import lax
from jax.experimental import pallas as pl
from jax.experimental.pallas import tpu as pltpu
from jax.sharding import Mesh, PartitionSpec as P

ROWS, COLS, C = 160, 80, 128
LANES = 128
REST = ROWS - LANES
PACK = LANES // REST
TAIL = COLS // PACK
CHUNK = 16
CHUNKS = COLS // CHUNK
STEP = CHUNK + 4
TAIL_STEP = 2 * TAIL + 4
COLS_STEP = COLS + 4
SPARE = 16
BOTH = 2 * (COLS + TAIL)
BACK = 104
N_ROW, N_CHAN = 8, 16
HALF = N_CHAN // 2
SIZES = {"y": 4, "z_lo": 2, "core": 2, "z_hi": 2, "x": 4}
ROW, CHAN = ("z_hi", "x"), ("y", "z_lo", "core")
OUT_ORDER = ("z_hi", "x", "core", "y", "z_lo")
BACK_ORDER = ("y", "x", "core", "z_lo", "z_hi")
SIDE = 1280
F32, BF16 = jnp.float32, jnp.bfloat16
MIB = 1 << 20
VMEM_BYTES = 36 * MIB


def places(order, inside):
    found = []
    for n in range(N_ROW * N_CHAN):
        at = {}
        for axis in reversed(inside):
            n, at[axis] = divmod(n, SIZES[axis])
        number = 0
        for axis in order:
            number = number * SIZES[axis] + at[axis]
        found.append(number)
    return found


OUT_OF_CHANNEL = places(OUT_ORDER, BACK_ORDER)
FROM_BLOCK = places(OUT_ORDER, ROW + CHAN)
BACK_TO_BLOCK = places(BACK_ORDER, ROW + CHAN)


def layer_norm(values, gain, bias, axis):
    mean = jnp.mean(values, axis=axis, keepdims=True)
    centred = values - mean
    var = jnp.mean(centred * centred, axis=axis, keepdims=True)
    return centred * lax.rsqrt(var + 1e-05) * gain + bias


def in_hbm(*arrays):
    return [pltpu.with_memory_space_constraint(array, pltpu.HBM) for array in arrays]


def fetch(sources, targets, sems):
    copies = [pltpu.make_async_copy(src, dst, sems.at[n]) for n, (src, dst) in enumerate(zip(sources, targets))]
    for copy in copies:
        copy.start()
    return copies


def edges_kernel(
    pair_ref, gain_hbm, bias_hbm, weight_hbm, out_ref, gain_ref, bias_ref, weight_ref, weight_t, held, normed, dense,
    tail, sems, small_sems
):
    small = fetch((gain_hbm, bias_hbm, weight_hbm), (gain_ref, bias_ref, weight_ref), small_sems)
    for t in range(CHUNKS):
        pltpu.make_async_copy(pair_ref.at[:, pl.ds(t * CHUNK, CHUNK), :], held.at[t], sems.at[t]).start()
    for copy in small:
        copy.wait()
    for m in range(4):
        columns = (0.5 * weight_ref[:, m * C : (m + 1) * C].astype(F32)).T.astype(BF16)
        for b in range(C // 16):
            at = 2 * C * (m // 2) + 32 * b + 16 * (m % 2)
            weight_t[at : at + 16, :] = columns[16 * b : 16 * b + 16]
    gain, bias = gain_ref[...], bias_ref[...]
    average = jnp.full((C, C), 1 / C, BF16)
    turn = lax.axis_index("x")

    def product(x, side):
        both = lax.dot_general(
            weight_t[side * 2 * C : (side + 1) * 2 * C, :], x, (((1,), (1,)), ((), ())), preferred_element_type=F32
        )
        both = both.reshape(C // 16, 2, 16, x.shape[0])
        return (both[:, 0] * jnp.tanh(both[:, 1]) + both[:, 0]).reshape(C, x.shape[0])

    @pl.loop(0, CHUNKS)
    def _(t):
        pltpu.make_async_copy(pair_ref.at[:, pl.ds(t * CHUNK, CHUNK), :], held.at[t], sems.at[t]).wait()
        group = 16
        for n in range(ROWS // group):
            block = held[t, n * group : (n + 1) * group].reshape(group * CHUNK, C)
            centred = block.astype(F32) - jnp.dot(block, average, preferred_element_type=F32)
            var = jnp.mean(centred * centred, axis=-1, keepdims=True)
            block = centred * lax.rsqrt(var + 1e-05) * gain + bias
            for u in range(group):
                at = (n * group + u) * STEP
                normed[at : at + CHUNK, :] = block[u * CHUNK : (u + 1) * CHUNK]
        for n in range(CHUNK // 2):
            x = jnp.concatenate(
                [normed[pl.ds(2 * n + e, LANES, stride=STEP), :] for e in range(2)], axis=0
            ).astype(BF16)
            for side in range(2):
                value = product(x, side)
                for e in range(2):
                    dense[side, pl.ds(2 * n + e, C, stride=STEP), :] = value[:, e * 128 : (e + 1) * 128]
        for n in range(CHUNK // 8):
            x = jnp.concatenate(
                [
                    normed[pl.ds(LANES * STEP + 8 * n + u + lax.rem(g + PACK - turn, PACK), REST, stride=STEP), :]
                    for u in (0, PACK)
                    for g in range(PACK)
                ],
                axis=0,
            ).astype(BF16)
            for side in range(2):
                value = product(x, side)
                for e in range(2):
                    at = side * TAIL + 4 * t + 2 * n + e
                    tail[pl.ds(at, C, stride=TAIL_STEP), :] = value[:, e * 128 : (e + 1) * 128]
        for h in range(C):
            for side in range(2):
                to = pl.multiple_of(side * COLS + t * CHUNK, CHUNK)
                out_ref[OUT_OF_CHANNEL[h], pl.ds(to, CHUNK), :] = dense[side, h * STEP : h * STEP + CHUNK, :].astype(BF16)

    for h in range(C):
        out_ref[OUT_OF_CHANNEL[h], 2 * COLS :, :] = tail[h * TAIL_STEP : h * TAIL_STEP + 2 * TAIL, :].astype(BF16)


def edges(pair, gain, bias, weight):
    vmem, hbm = pl.BlockSpec(memory_space=pltpu.VMEM), pl.BlockSpec(memory_space=pltpu.HBM)
    return pl.pallas_call(
        edges_kernel,
        in_specs=[hbm] * 4,
        out_specs=vmem,
        out_shape=jax.ShapeDtypeStruct((C, BOTH, LANES), BF16),
        scratch_shapes=[
            pltpu.VMEM((1, C), F32),
            pltpu.VMEM((1, C), F32),
            pltpu.VMEM((C, 4 * C), BF16),
            pltpu.VMEM((4 * C, C), BF16),
            pltpu.VMEM((CHUNKS, ROWS, CHUNK, C), BF16),
            pltpu.VMEM((ROWS * STEP, C), F32),
            pltpu.VMEM((2, C * STEP, LANES), F32),
            pltpu.VMEM((C * TAIL_STEP, LANES), F32),
            pltpu.SemaphoreType.DMA((CHUNKS,)),
            pltpu.SemaphoreType.DMA((3,)),
        ],
        compiler_params=pltpu.CompilerParams(vmem_limit_bytes=VMEM_BYTES),
        cost_estimate=pl.CostEstimate(flops=2 * ROWS * COLS * C * 4 * C, bytes_accessed=10 * MIB, transcendentals=0),
        name="edges",
    )(*in_hbm(pair, gain[None, :], bias[None, :], weight))


def gate_kernel(
    pair_ref, gain_hbm, bias_hbm, weight_hbm, out_hbm, gain_ref, bias_ref, weight_ref, held, out_ref, sems
):
    for copy in fetch((pair_ref, gain_hbm, bias_hbm, weight_hbm), (held, gain_ref, bias_ref, weight_ref), sems):
        copy.wait()
    gain, bias, weight = gain_ref[...], bias_ref[...], weight_ref[...]
    group = 4

    @pl.loop(0, ROWS // group, unroll=2)
    def _(n):
        block = held[pl.ds(n * group, group)].reshape(group * COLS, C).astype(F32)
        normed = layer_norm(block, gain, bias, -1).astype(BF16)
        value = jax.nn.sigmoid(jnp.dot(normed, weight, preferred_element_type=F32))
        out_ref[pl.ds(n * group, group)] = value.astype(BF16).reshape(group, COLS, C)

    store = pltpu.make_async_copy(out_ref, out_hbm, sems.at[4])
    store.start()
    store.wait()


def gates(pair, gain, bias, weight):
    hbm = pl.BlockSpec(memory_space=pltpu.HBM)
    return pl.pallas_call(
        gate_kernel,
        in_specs=[hbm] * 4,
        out_specs=hbm,
        out_shape=pltpu.HBM((ROWS, COLS, C), BF16),
        scratch_shapes=[
            pltpu.VMEM((1, C), F32),
            pltpu.VMEM((1, C), F32),
            pltpu.VMEM((C, C), BF16),
            pltpu.VMEM((ROWS, COLS, C), BF16),
            pltpu.VMEM((ROWS, COLS, C), BF16),
            pltpu.SemaphoreType.DMA((5,)),
        ],
        compiler_params=pltpu.CompilerParams(vmem_limit_bytes=VMEM_BYTES),
        cost_estimate=pl.CostEstimate(flops=2 * ROWS * COLS * C * C, bytes_accessed=30 * MIB, transcendentals=0),
        name="gates",
    )(*in_hbm(pair, gain[None, :], bias[None, :], weight))


def choose(lane, pieces):
    out = pieces[0]
    for g in range(1, PACK):
        out = jnp.where(lane // REST == g, pieces[g], out)
    return out


def turned(value, groups):
    return pltpu.roll(value, groups * REST, 1) if groups else value


def triangle_kernel(edges_ref, out_hbm, left_rest, right_t, rest_left, rest_right, tri_rest, out_ref, sem):
    lane = lax.broadcasted_iota(jnp.int32, (2 * TAIL, LANES), 1)
    for c in range(N_CHAN):
        for q in range(N_ROW // PACK):
            blocks = [FROM_BLOCK[(q * PACK + a) * N_CHAN + c] for a in range(PACK)]
            pieces = [edges_ref[block, 2 * COLS :, :].astype(F32) for block in blocks]
            for b in range(PACK):
                value = turned(choose(lane, [pieces[(g - b) % PACK] for g in range(PACK)]), -b % PACK)
                rest_left[q, pl.ds(c * COLS + b, TAIL, stride=PACK), :] = value[:TAIL]
                rest_right[q, pl.ds(c * COLS + b, TAIL, stride=PACK), :] = value[TAIL:]

    def side(r, first):
        blocks = FROM_BLOCK[r * N_CHAN : (r + 1) * N_CHAN]
        return jnp.concatenate([edges_ref[block, first : first + COLS, :] for block in blocks], axis=0)

    for q in range(N_ROW // PACK):
        left_rest[:, q * LANES : (q + 1) * LANES] = rest_left[q, :SIDE].astype(BF16)
        columns = rest_right[q, :SIDE].astype(BF16).T
        for a in range(PACK):
            at = (q * PACK + a) * ROWS + LANES
            right_t[at : at + REST, :] = columns[a * REST : (a + 1) * REST]
    for r in range(N_ROW):
        right_t[r * ROWS : r * ROWS + LANES, :] = side(r, COLS).T

    for first in range(0, N_CHAN, HALF):
        rows = pl.ds(first * COLS, HALF * COLS)
        part = jnp.dot(right_t[rows, :], left_rest[...], preferred_element_type=F32)
        for q in range(N_ROW // PACK):
            tri_rest[q, rows, :] = part[:, q * LANES : (q + 1) * LANES]
    lane = lax.broadcasted_iota(jnp.int32, (TAIL, LANES), 1)
    for n in range(N_ROW // 2):
        q = n // 2
        if n % 2 == 0:
            for c in range(N_CHAN):
                pieces = [tri_rest[q, pl.ds(c * COLS + b, TAIL, stride=PACK), :] for b in range(PACK)]
                pieces = [turned(piece, b) for b, piece in enumerate(pieces)]
                for a in range(PACK):
                    value = choose(lane, [pieces[(g - a) % PACK] for g in range(PACK)])
                    value = jnp.concatenate([value, jnp.zeros((BACK - COLS - TAIL, LANES), F32)], axis=0)
                    out_ref[BACK_TO_BLOCK[(q * PACK + a) * N_CHAN + c], COLS:, :] = value.astype(BF16)
        pair = jnp.concatenate([side(2 * n, 0), side(2 * n + 1, 0)], axis=1)
        for first in range(0, N_CHAN, HALF):
            rows = right_t[first * COLS : (first + HALF) * COLS]
            part = jnp.dot(rows, pair, preferred_element_type=F32).astype(BF16)
            for e in range(2):
                for c in range(HALF):
                    to = BACK_TO_BLOCK[(2 * n + e) * N_CHAN + first + c]
                    out_ref[to, :COLS, :] = part[c * COLS : (c + 1) * COLS, e * LANES : (e + 1) * LANES]
                    pltpu.make_async_copy(out_ref.at[to], out_hbm.at[to], sem).start()
    pltpu.make_async_copy(out_ref, out_hbm, sem).wait()


def triangle(edges_all):
    vmem = pl.BlockSpec(memory_space=pltpu.VMEM)
    return pl.pallas_call(
        triangle_kernel,
        in_specs=[vmem],
        out_specs=pl.BlockSpec(memory_space=pltpu.HBM),
        out_shape=pltpu.HBM((N_ROW * N_CHAN, BACK, LANES), BF16),
        scratch_shapes=[
            pltpu.VMEM((SIDE, 2 * LANES), BF16),
            pltpu.VMEM((SIDE, SIDE), BF16),
            pltpu.VMEM((N_ROW // PACK, SIDE + SPARE, LANES), F32),
            pltpu.VMEM((N_ROW // PACK, SIDE + SPARE, LANES), F32),
            pltpu.VMEM((N_ROW // PACK, SIDE + SPARE, LANES), F32),
            pltpu.VMEM((N_ROW * N_CHAN, BACK, LANES), BF16),
            pltpu.SemaphoreType.DMA,
        ],
        compiler_params=pltpu.CompilerParams(vmem_limit_bytes=VMEM_BYTES),
        cost_estimate=pl.CostEstimate(flops=2 * SIDE**3, bytes_accessed=10 * MIB, transcendentals=0),
        name="triangle",
    )(edges_all)


def finish_kernel(
    held, gate_hbm, gain_hbm, bias_hbm, weight_hbm, out_ref, gate_ref, gain_ref, bias_ref, weight_ref, wide, dense, tail, done,
    sems, small_sems
):
    def store(t):
        rows = pl.ds(pl.multiple_of(t * CHUNK, CHUNK), CHUNK)
        return pltpu.make_async_copy(
            done.at[pl.ds(0, LANES), rows, :], out_ref.at[pl.ds(0, LANES), rows, :], sems.at[CHUNKS + 1]
        )

    def load(t):
        rows = pl.ds(pl.multiple_of(t * CHUNK, CHUNK), CHUNK)
        return pltpu.make_async_copy(
            gate_hbm.at[pl.ds(0, LANES), rows, :], gate_ref.at[pl.ds(0, LANES), rows, :], sems.at[t]
        )

    rest = pl.ds(LANES, REST)
    small = fetch((gain_hbm, bias_hbm, weight_hbm), (gain_ref, bias_ref, weight_ref), small_sems)
    gate_tail = pltpu.make_async_copy(gate_hbm.at[rest], gate_ref.at[rest], sems.at[CHUNKS])
    gate_tail.start()
    for t in range(CHUNKS):
        load(t).start()
    turn = lax.axis_index("x")
    for h in range(C):
        wide[h * STEP : h * STEP + TAIL, :] = held[h, COLS:, :].astype(F32)[:TAIL]
    for copy in small:
        copy.wait()
    gain = jnp.broadcast_to(gain_ref[...], (LANES, C)).T
    bias = jnp.broadcast_to(bias_ref[...], (LANES, C)).T
    weight = weight_ref[...]

    def project(g):
        normed = layer_norm(wide[pl.ds(g, C, stride=STEP), :], gain, bias, 0).astype(BF16)
        return lax.dot_general(normed, weight, (((0,), (0,)), ((), ())), preferred_element_type=F32)

    for m in range(TAIL):
        value = project(m)
        for g in range(PACK):
            at = PACK * m + lax.rem(g + PACK - turn, PACK)
            tail[pl.ds(at, REST, stride=COLS_STEP), :] = value[g * REST : (g + 1) * REST]
    gate_tail.wait()
    for i in range(REST):
        gate = gate_ref[LANES + i].astype(F32)
        done[LANES + i] = (gate * tail[i * COLS_STEP : i * COLS_STEP + COLS, :]).astype(BF16)
    last = pltpu.make_async_copy(done.at[rest], out_ref.at[rest], sems.at[CHUNKS + 2])
    last.start()

    @pl.loop(0, CHUNKS)
    def _(t):
        load(t).wait()
        to = pl.multiple_of(t * CHUNK, CHUNK)
        for h in range(C):
            wide[h * STEP : h * STEP + CHUNK, :] = held[h, pl.ds(to, CHUNK), :].astype(F32)
        for g in range(CHUNK):
            dense[pl.ds(g, LANES, stride=STEP), :] = project(g)
        for i in range(LANES):
            gate = gate_ref[i, pl.ds(to, CHUNK), :].astype(F32)
            done[i, pl.ds(to, CHUNK), :] = (gate * dense[i * STEP : i * STEP + CHUNK, :]).astype(BF16)
        store(t).start()

    last.wait()
    for t in range(CHUNKS):
        store(t).wait()


def finish(tri, gate, gain, bias, weight):
    vmem, hbm = pl.BlockSpec(memory_space=pltpu.VMEM), pl.BlockSpec(memory_space=pltpu.HBM)
    return pl.pallas_call(
        finish_kernel,
        in_specs=[vmem, hbm, hbm, hbm, hbm],
        out_specs=hbm,
        out_shape=jax.ShapeDtypeStruct((ROWS, COLS, C), BF16),
        scratch_shapes=[
            pltpu.VMEM((ROWS, COLS, C), BF16),
            pltpu.VMEM((1, C), F32),
            pltpu.VMEM((1, C), F32),
            pltpu.VMEM((C, C), BF16),
            pltpu.VMEM((C * STEP + SPARE, LANES), F32),
            pltpu.VMEM((LANES * STEP, C), F32),
            pltpu.VMEM((REST * COLS_STEP, C), F32),
            pltpu.VMEM((ROWS, COLS, C), BF16),
            pltpu.SemaphoreType.DMA((CHUNKS + 3,)),
            pltpu.SemaphoreType.DMA((3,)),
        ],
        compiler_params=pltpu.CompilerParams(vmem_limit_bytes=VMEM_BYTES),
        cost_estimate=pl.CostEstimate(flops=2 * ROWS * COLS * C * C, bytes_accessed=10 * MIB, transcendentals=0),
        name="finish",
    )(tri, *in_hbm(gate, gain[None, :], bias[None, :], weight))


def shards(pair, in_gain, in_bias, edge_weight, gate_weight, out_gain, out_bias, out_weight):
    both = edges(pair, in_gain, in_bias, edge_weight)
    both_all = lax.all_to_all(both, OUT_ORDER, split_axis=0, concat_axis=0, tiled=True)
    gate = gates(pair, in_gain, in_bias, gate_weight)
    tri = lax.all_to_all(triangle(both_all), BACK_ORDER, split_axis=0, concat_axis=0, tiled=True)
    return finish(tri, gate, out_gain, out_bias, out_weight)


def solution(mesh):
    apart = Mesh(mesh.devices.reshape(tuple(SIZES.values())), tuple(SIZES))
    return jax.shard_map(
        shards,
        mesh=apart,
        in_specs=(P(ROW, CHAN, None), P(), P(), P(), P(), P(), P(), P()),
        out_specs=P(ROW, CHAN, None),
        check_vma=False,
    )
```

```python
import jax
import jax.numpy as jnp
from jax import lax
from jax.experimental import pallas as pl
from jax.experimental.pallas import tpu as pltpu
from jax.sharding import Mesh, PartitionSpec as P

ROWS, COLS, C = 160, 80, 128
LANES = 128
REST = ROWS - LANES
PACK = LANES // REST
TAIL = COLS // PACK
CHUNK = 16
CHUNKS = COLS // CHUNK
STEP = CHUNK + 4
TAIL_STEP = 2 * TAIL + 4
COLS_STEP = COLS + 4
SPARE = 16
BOTH = 2 * (COLS + TAIL)
BACK = 104
N_ROW, N_CHAN = 8, 16
HALF = N_CHAN // 2
SIZES = {"y": 4, "z_lo": 2, "core": 2, "z_hi": 2, "x": 4}
ROW, CHAN = ("z_hi", "x"), ("y", "z_lo", "core")
OUT_ORDER = ("z_hi", "x", "core", "y", "z_lo")
BACK_ORDER = ("y", "x", "core", "z_lo", "z_hi")
SIDE = 1280
F32, BF16 = jnp.float32, jnp.bfloat16
MIB = 1 << 20
VMEM_BYTES = 36 * MIB


def places(order, inside):
    found = []
    for n in range(N_ROW * N_CHAN):
        at = {}
        for axis in reversed(inside):
            n, at[axis] = divmod(n, SIZES[axis])
        number = 0
        for axis in order:
            number = number * SIZES[axis] + at[axis]
        found.append(number)
    return found


OUT_OF_CHANNEL = places(OUT_ORDER, BACK_ORDER)
FROM_BLOCK = places(OUT_ORDER, ROW + CHAN)
BACK_TO_BLOCK = places(BACK_ORDER, ROW + CHAN)


def layer_norm(values, gain, bias, axis):
    mean = jnp.mean(values, axis=axis, keepdims=True)
    centred = values - mean
    var = jnp.mean(centred * centred, axis=axis, keepdims=True)
    return centred * lax.rsqrt(var + 1e-05) * gain + bias


def in_hbm(*arrays):
    return [pltpu.with_memory_space_constraint(array, pltpu.HBM) for array in arrays]


def fetch(sources, targets, sems):
    copies = [pltpu.make_async_copy(src, dst, sems.at[n]) for n, (src, dst) in enumerate(zip(sources, targets))]
    for copy in copies:
        copy.start()
    return copies


def edges_kernel(
    pair_ref, gain_hbm, bias_hbm, weight_hbm, out_ref, gain_ref, bias_ref, weight_ref, weight_t, held, normed, dense,
    tail, sems, small_sems
):
    small = fetch((gain_hbm, bias_hbm, weight_hbm), (gain_ref, bias_ref, weight_ref), small_sems)
    for t in range(CHUNKS):
        pltpu.make_async_copy(pair_ref.at[:, pl.ds(t * CHUNK, CHUNK), :], held.at[t], sems.at[t]).start()
    for copy in small:
        copy.wait()
    for m in range(4):
        columns = (0.5 * weight_ref[:, m * C : (m + 1) * C].astype(F32)).T.astype(BF16)
        for b in range(C // 16):
            at = 2 * C * (m // 2) + 32 * b + 16 * (m % 2)
            weight_t[at : at + 16, :] = columns[16 * b : 16 * b + 16]
    gain, bias = gain_ref[...], bias_ref[...]
    average = jnp.full((C, C), 1 / C, BF16)
    turn = lax.axis_index("x")

    def product(x, side):
        both = lax.dot_general(
            weight_t[side * 2 * C : (side + 1) * 2 * C, :], x, (((1,), (1,)), ((), ())), preferred_element_type=F32
        )
        both = both.reshape(C // 16, 2, 16, x.shape[0])
        return (both[:, 0] * jnp.tanh(both[:, 1]) + both[:, 0]).reshape(C, x.shape[0])

    @pl.loop(0, CHUNKS)
    def _(t):
        pltpu.make_async_copy(pair_ref.at[:, pl.ds(t * CHUNK, CHUNK), :], held.at[t], sems.at[t]).wait()
        group = 16
        for n in range(ROWS // group):
            block = held[t, n * group : (n + 1) * group].reshape(group * CHUNK, C)
            centred = block.astype(F32) - jnp.dot(block, average, preferred_element_type=F32)
            var = jnp.mean(centred * centred, axis=-1, keepdims=True)
            block = centred * lax.rsqrt(var + 1e-05) * gain + bias
            for u in range(group):
                at = (n * group + u) * STEP
                normed[at : at + CHUNK, :] = block[u * CHUNK : (u + 1) * CHUNK]
        for n in range(CHUNK // 2):
            x = jnp.concatenate(
                [normed[pl.ds(2 * n + e, LANES, stride=STEP), :] for e in range(2)], axis=0
            ).astype(BF16)
            for side in range(2):
                value = product(x, side)
                for e in range(2):
                    dense[side, pl.ds(2 * n + e, C, stride=STEP), :] = value[:, e * 128 : (e + 1) * 128]
        for n in range(CHUNK // 8):
            x = jnp.concatenate(
                [
                    normed[pl.ds(LANES * STEP + 8 * n + u + lax.rem(g + PACK - turn, PACK), REST, stride=STEP), :]
                    for u in (0, PACK)
                    for g in range(PACK)
                ],
                axis=0,
            ).astype(BF16)
            for side in range(2):
                value = product(x, side)
                for e in range(2):
                    at = side * TAIL + 4 * t + 2 * n + e
                    tail[pl.ds(at, C, stride=TAIL_STEP), :] = value[:, e * 128 : (e + 1) * 128]
        for h in range(C):
            for side in range(2):
                to = pl.multiple_of(side * COLS + t * CHUNK, CHUNK)
                out_ref[OUT_OF_CHANNEL[h], pl.ds(to, CHUNK), :] = dense[side, h * STEP : h * STEP + CHUNK, :].astype(BF16)

    for h in range(C):
        out_ref[OUT_OF_CHANNEL[h], 2 * COLS :, :] = tail[h * TAIL_STEP : h * TAIL_STEP + 2 * TAIL, :].astype(BF16)


def edges(pair, gain, bias, weight):
    vmem, hbm = pl.BlockSpec(memory_space=pltpu.VMEM), pl.BlockSpec(memory_space=pltpu.HBM)
    return pl.pallas_call(
        edges_kernel,
        in_specs=[hbm] * 4,
        out_specs=vmem,
        out_shape=jax.ShapeDtypeStruct((C, BOTH, LANES), BF16),
        scratch_shapes=[
            pltpu.VMEM((1, C), F32),
            pltpu.VMEM((1, C), F32),
            pltpu.VMEM((C, 4 * C), BF16),
            pltpu.VMEM((4 * C, C), BF16),
            pltpu.VMEM((CHUNKS, ROWS, CHUNK, C), BF16),
            pltpu.VMEM((ROWS * STEP, C), F32),
            pltpu.VMEM((2, C * STEP, LANES), F32),
            pltpu.VMEM((C * TAIL_STEP, LANES), F32),
            pltpu.SemaphoreType.DMA((CHUNKS,)),
            pltpu.SemaphoreType.DMA((3,)),
        ],
        compiler_params=pltpu.CompilerParams(vmem_limit_bytes=VMEM_BYTES),
        cost_estimate=pl.CostEstimate(flops=2 * ROWS * COLS * C * 4 * C, bytes_accessed=10 * MIB, transcendentals=0),
        name="edges",
    )(*in_hbm(pair, gain[None, :], bias[None, :], weight))


def gate_kernel(
    pair_ref, gain_hbm, bias_hbm, weight_hbm, out_hbm, gain_ref, bias_ref, weight_ref, held, out_ref, sems
):
    for copy in fetch((pair_ref, gain_hbm, bias_hbm, weight_hbm), (held, gain_ref, bias_ref, weight_ref), sems):
        copy.wait()
    gain, bias, weight = gain_ref[...], bias_ref[...], weight_ref[...]
    group = 4

    @pl.loop(0, ROWS // group, unroll=2)
    def _(n):
        block = held[pl.ds(n * group, group)].reshape(group * COLS, C).astype(F32)
        normed = layer_norm(block, gain, bias, -1).astype(BF16)
        value = jax.nn.sigmoid(jnp.dot(normed, weight, preferred_element_type=F32))
        out_ref[pl.ds(n * group, group)] = value.astype(BF16).reshape(group, COLS, C)

    store = pltpu.make_async_copy(out_ref, out_hbm, sems.at[4])
    store.start()
    store.wait()


def gates(pair, gain, bias, weight):
    hbm = pl.BlockSpec(memory_space=pltpu.HBM)
    return pl.pallas_call(
        gate_kernel,
        in_specs=[hbm] * 4,
        out_specs=hbm,
        out_shape=pltpu.HBM((ROWS, COLS, C), BF16),
        scratch_shapes=[
            pltpu.VMEM((1, C), F32),
            pltpu.VMEM((1, C), F32),
            pltpu.VMEM((C, C), BF16),
            pltpu.VMEM((ROWS, COLS, C), BF16),
            pltpu.VMEM((ROWS, COLS, C), BF16),
            pltpu.SemaphoreType.DMA((5,)),
        ],
        compiler_params=pltpu.CompilerParams(vmem_limit_bytes=VMEM_BYTES),
        cost_estimate=pl.CostEstimate(flops=2 * ROWS * COLS * C * C, bytes_accessed=30 * MIB, transcendentals=0),
        name="gates",
    )(*in_hbm(pair, gain[None, :], bias[None, :], weight))


def choose(lane, pieces):
    out = pieces[0]
    for g in range(1, PACK):
        out = jnp.where(lane // REST == g, pieces[g], out)
    return out


def turned(value, groups):
    return pltpu.roll(value, groups * REST, 1) if groups else value


def triangle_kernel(edges_ref, out_hbm, left_rest, right_t, rest_left, rest_right, tri_rest, out_ref, sem):
    lane = lax.broadcasted_iota(jnp.int32, (2 * TAIL, LANES), 1)
    for c in range(N_CHAN):
        for q in range(N_ROW // PACK):
            blocks = [FROM_BLOCK[(q * PACK + a) * N_CHAN + c] for a in range(PACK)]
            pieces = [edges_ref[block, 2 * COLS :, :].astype(F32) for block in blocks]
            for b in range(PACK):
                value = turned(choose(lane, [pieces[(g - b) % PACK] for g in range(PACK)]), -b % PACK)
                rest_left[q, pl.ds(c * COLS + b, TAIL, stride=PACK), :] = value[:TAIL]
                rest_right[q, pl.ds(c * COLS + b, TAIL, stride=PACK), :] = value[TAIL:]

    def side(r, first):
        blocks = FROM_BLOCK[r * N_CHAN : (r + 1) * N_CHAN]
        return jnp.concatenate([edges_ref[block, first : first + COLS, :] for block in blocks], axis=0)

    for q in range(N_ROW // PACK):
        left_rest[:, q * LANES : (q + 1) * LANES] = rest_left[q, :SIDE].astype(BF16)
        columns = rest_right[q, :SIDE].astype(BF16).T
        for a in range(PACK):
            at = (q * PACK + a) * ROWS + LANES
            right_t[at : at + REST, :] = columns[a * REST : (a + 1) * REST]
    for r in range(N_ROW):
        right_t[r * ROWS : r * ROWS + LANES, :] = side(r, COLS).T

    for first in range(0, N_CHAN, HALF):
        rows = pl.ds(first * COLS, HALF * COLS)
        part = jnp.dot(right_t[rows, :], left_rest[...], preferred_element_type=F32)
        for q in range(N_ROW // PACK):
            tri_rest[q, rows, :] = part[:, q * LANES : (q + 1) * LANES]
    lane = lax.broadcasted_iota(jnp.int32, (TAIL, LANES), 1)
    for n in range(N_ROW // 2):
        q = n // 2
        if n % 2 == 0:
            for c in range(N_CHAN):
                pieces = [tri_rest[q, pl.ds(c * COLS + b, TAIL, stride=PACK), :] for b in range(PACK)]
                pieces = [turned(piece, b) for b, piece in enumerate(pieces)]
                for a in range(PACK):
                    value = choose(lane, [pieces[(g - a) % PACK] for g in range(PACK)])
                    value = jnp.concatenate([value, jnp.zeros((BACK - COLS - TAIL, LANES), F32)], axis=0)
                    out_ref[BACK_TO_BLOCK[(q * PACK + a) * N_CHAN + c], COLS:, :] = value.astype(BF16)
        pair = jnp.concatenate([side(2 * n, 0), side(2 * n + 1, 0)], axis=1)
        for first in range(0, N_CHAN, HALF):
            rows = right_t[first * COLS : (first + HALF) * COLS]
            part = jnp.dot(rows, pair, preferred_element_type=F32).astype(BF16)
            for e in range(2):
                for c in range(HALF):
                    to = BACK_TO_BLOCK[(2 * n + e) * N_CHAN + first + c]
                    out_ref[to, :COLS, :] = part[c * COLS : (c + 1) * COLS, e * LANES : (e + 1) * LANES]
                    pltpu.make_async_copy(out_ref.at[to], out_hbm.at[to], sem).start()
    pltpu.make_async_copy(out_ref, out_hbm, sem).wait()


def triangle(edges_all):
    vmem = pl.BlockSpec(memory_space=pltpu.VMEM)
    return pl.pallas_call(
        triangle_kernel,
        in_specs=[vmem],
        out_specs=pl.BlockSpec(memory_space=pltpu.HBM),
        out_shape=pltpu.HBM((N_ROW * N_CHAN, BACK, LANES), BF16),
        scratch_shapes=[
            pltpu.VMEM((SIDE, 2 * LANES), BF16),
            pltpu.VMEM((SIDE, SIDE), BF16),
            pltpu.VMEM((N_ROW // PACK, SIDE + SPARE, LANES), F32),
            pltpu.VMEM((N_ROW // PACK, SIDE + SPARE, LANES), F32),
            pltpu.VMEM((N_ROW // PACK, SIDE + SPARE, LANES), F32),
            pltpu.VMEM((N_ROW * N_CHAN, BACK, LANES), BF16),
            pltpu.SemaphoreType.DMA,
        ],
        compiler_params=pltpu.CompilerParams(vmem_limit_bytes=VMEM_BYTES),
        cost_estimate=pl.CostEstimate(flops=2 * SIDE**3, bytes_accessed=10 * MIB, transcendentals=0),
        name="triangle",
    )(edges_all)


def finish_kernel(
    held, gate_hbm, gain_hbm, bias_hbm, weight_hbm, out_ref, gate_ref, gain_ref, bias_ref, weight_ref, wide, dense, tail, done,
    sems, small_sems
):
    def store(t):
        rows = pl.ds(t * CHUNK, CHUNK)
        return pltpu.make_async_copy(
            done.at[pl.ds(0, LANES), rows, :], out_ref.at[pl.ds(0, LANES), rows, :], sems.at[CHUNKS + 1]
        )

    def load(t):
        rows = pl.ds(t * CHUNK, CHUNK)
        return pltpu.make_async_copy(
            gate_hbm.at[pl.ds(0, LANES), rows, :], gate_ref.at[pl.ds(0, LANES), rows, :], sems.at[t]
        )

    rest = pl.ds(LANES, REST)
    small = fetch((gain_hbm, bias_hbm, weight_hbm), (gain_ref, bias_ref, weight_ref), small_sems)
    gate_tail = pltpu.make_async_copy(gate_hbm.at[rest], gate_ref.at[rest], sems.at[CHUNKS])
    gate_tail.start()
    for t in range(CHUNKS):
        load(t).start()
    turn = lax.axis_index("x")
    for h in range(C):
        wide[1, h * STEP : h * STEP + TAIL, :] = held[h, COLS:, :].astype(F32)[:TAIL]
    for copy in small:
        copy.wait()
    gain = jnp.broadcast_to(gain_ref[...], (LANES, C)).T
    bias = jnp.broadcast_to(bias_ref[...], (LANES, C)).T
    weight = weight_ref[...]

    def project(g, slot):
        normed = layer_norm(wide[slot, pl.ds(g, C, stride=STEP), :], gain, bias, 0).astype(BF16)
        return lax.dot_general(normed, weight, (((0,), (0,)), ((), ())), preferred_element_type=F32)

    for m in range(TAIL):
        value = project(m, 1)
        for g in range(PACK):
            at = PACK * m + lax.rem(g + PACK - turn, PACK)
            tail[pl.ds(at, REST, stride=COLS_STEP), :] = value[g * REST : (g + 1) * REST]
    gate_tail.wait()
    for i in range(REST):
        gate = gate_ref[LANES + i].astype(F32)
        done[LANES + i] = (gate * tail[i * COLS_STEP : i * COLS_STEP + COLS, :]).astype(BF16)
    last = pltpu.make_async_copy(done.at[rest], out_ref.at[rest], sems.at[CHUNKS + 2])
    last.start()

    for t in range(CHUNKS):
        to, slot = t * CHUNK, t % 2
        for h in range(C):
            wide[slot, h * STEP : h * STEP + CHUNK, :] = held[h, pl.ds(to, CHUNK), :].astype(F32)
        for g in range(CHUNK):
            dense[slot, pl.ds(g, LANES, stride=STEP), :] = project(g, slot)
        load(t).wait()
        for i in range(LANES):
            gate = gate_ref[i, pl.ds(to, CHUNK), :].astype(F32)
            done[i, pl.ds(to, CHUNK), :] = (gate * dense[slot, i * STEP : i * STEP + CHUNK, :]).astype(BF16)
        store(t).start()

    last.wait()
    for t in range(CHUNKS):
        store(t).wait()


def finish(tri, gate, gain, bias, weight):
    vmem, hbm = pl.BlockSpec(memory_space=pltpu.VMEM), pl.BlockSpec(memory_space=pltpu.HBM)
    return pl.pallas_call(
        finish_kernel,
        in_specs=[vmem, hbm, hbm, hbm, hbm],
        out_specs=hbm,
        out_shape=jax.ShapeDtypeStruct((ROWS, COLS, C), BF16),
        scratch_shapes=[
            pltpu.VMEM((ROWS, COLS, C), BF16),
            pltpu.VMEM((1, C), F32),
            pltpu.VMEM((1, C), F32),
            pltpu.VMEM((C, C), BF16),
            pltpu.VMEM((2, C * STEP + SPARE, LANES), F32),
            pltpu.VMEM((2, LANES * STEP, C), F32),
            pltpu.VMEM((REST * COLS_STEP, C), F32),
            pltpu.VMEM((ROWS, COLS, C), BF16),
            pltpu.SemaphoreType.DMA((CHUNKS + 3,)),
            pltpu.SemaphoreType.DMA((3,)),
        ],
        compiler_params=pltpu.CompilerParams(vmem_limit_bytes=VMEM_BYTES),
        cost_estimate=pl.CostEstimate(flops=2 * ROWS * COLS * C * C, bytes_accessed=10 * MIB, transcendentals=0),
        name="finish",
    )(tri, *in_hbm(gate, gain[None, :], bias[None, :], weight))


def shards(pair, in_gain, in_bias, edge_weight, gate_weight, out_gain, out_bias, out_weight):
    both = edges(pair, in_gain, in_bias, edge_weight)
    both_all = lax.all_to_all(both, OUT_ORDER, split_axis=0, concat_axis=0, tiled=True)
    gate = gates(pair, in_gain, in_bias, gate_weight)
    tri = lax.all_to_all(triangle(both_all), BACK_ORDER, split_axis=0, concat_axis=0, tiled=True)
    return finish(tri, gate, out_gain, out_bias, out_weight)


def solution(mesh):
    apart = Mesh(mesh.devices.reshape(tuple(SIZES.values())), tuple(SIZES))
    return jax.shard_map(
        shards,
        mesh=apart,
        in_specs=(P(ROW, CHAN, None), P(), P(), P(), P(), P(), P(), P()),
        out_specs=P(ROW, CHAN, None),
        check_vma=False,
    )
```
